32 devices in a mesh: dp: 4 (over y, x), seq: 8 (over z, core).
Axes of the slice: x: 2, y: 2, z: 4, core: 2. Of those that a mesh axis runs over, the one named last changes fastest.
Arguments:
- tokens: bfloat16 [32768, 1024], P(('dp', 'seq')), may hold values from -6 to 6
- seg_starts: int32 [32768], P(('dp', 'seq')), may hold values from 0 to 1, as said below
- cotangent: bfloat16 [32768, 1024], P(('dp', 'seq')), may hold values from -6 to 6
- recur_in: bfloat16 [1024, 1536], P(('dp', 'seq')), may hold values from -0.1875 to 0.1875
- gelu_branch: bfloat16 [1024, 1536], P(('dp', 'seq')), may hold values from -0.1875 to 0.1875
- mixer_out: bfloat16 [1536, 1024], P(('dp', 'seq')), may hold values from -0.625 to 0.625
- conv_weight: bfloat16 [4, 1536], P(None, ('dp', 'seq')), may hold values from -3 to 3
- conv_bias: bfloat16 [1536], P(('dp', 'seq')), may hold values from -3 to 3
- rate_gate: bfloat16 [1536, 128], P(('dp', 'seq')), may hold values from -0.5 to 0.5
- input_gate: bfloat16 [1536, 128], P(('dp', 'seq')), may hold values from -0.5 to 0.5
- rate_bias: bfloat16 [1536], P(('dp', 'seq')), may hold values from -4 to 4
- input_bias: bfloat16 [1536], P(('dp', 'seq')), may hold values from -4 to 4
- decay_param: bfloat16 [1536], P(('dp', 'seq')), may hold values from 4 to 16
- mixer_gain: bfloat16 [1024], P(('dp', 'seq')), may hold values from 0.5 to 1.5
- mlp_gate: bfloat16 [1024, 3072], P(('dp', 'seq')), may hold values from -0.1875 to 0.1875
- mlp_up: bfloat16 [1024, 3072], P(('dp', 'seq')), may hold values from -0.1875 to 0.1875
- mlp_down: bfloat16 [3072, 1024], P(('dp', 'seq')), may hold values from -0.21875 to 0.21875
- mlp_gain: bfloat16 [1024], P(('dp', 'seq')), may hold values from 0.5 to 1.5
Outputs:
- block_out: bfloat16 [32768, 1024], P(('dp', 'seq'))
- tokens_grad: bfloat16 [32768, 1024], P(('dp', 'seq'))
- recur_in_grad: float32 [1024, 1536], P(('dp', 'seq'))
- gelu_branch_grad: float32 [1024, 1536], P(('dp', 'seq'))
- mixer_out_grad: float32 [1536, 1024], P(('dp', 'seq'))
- conv_weight_grad: float32 [4, 1536], P(None, ('dp', 'seq'))
- conv_bias_grad: float32 [1536], P(('dp', 'seq'))
- rate_gate_grad: float32 [1536, 128], P(('dp', 'seq'))
- input_gate_grad: float32 [1536, 128], P(('dp', 'seq'))
- rate_bias_grad: float32 [1536], P(('dp', 'seq'))
- input_bias_grad: float32 [1536], P(('dp', 'seq'))
- decay_param_grad: float32 [1536], P(('dp', 'seq'))
- mixer_gain_grad: float32 [1024], P(('dp', 'seq'))
- mlp_gate_grad: float32 [1024, 3072], P(('dp', 'seq'))
- mlp_up_grad: float32 [1024, 3072], P(('dp', 'seq'))
- mlp_down_grad: float32 [3072, 1024], P(('dp', 'seq'))
- mlp_gain_grad: float32 [1024], P(('dp', 'seq'))
The draws below stay inside these ranges and needn't reach their ends.
Inputs may be any that keep to these rules, and one draw needn't show every extreme that they name: `seg_starts`: values 0 or 1. Starts mark the row boundaries of a packing of rows. The first token of each group of 8192 is a start. In each group one long row begins within the group's first 1024 tokens and ends within its last 1024 tokens. Before and after it the group is packed with rows of 512 tokens, the row at the group's start and the row at its end being partial.
All inputs are finite; a program needn't handle non-finite values.
Results may differ from the reference program's by a relative error of at most 0.011.
Values may be sent and summed in bfloat16 or wider, within the bound.
No kernel may reach another device: no remote copies, remote signals or barrier semaphores. Data moves between devices by JAX's collectives and lax.ppermute only.
A program may use at most 256 MiB of HBM per device.

```python
import math
import jax
import jax.numpy as jnp
from jax import lax

D = 1024
LRU = 1536
FF = 3072
CONV = 4
HEADS = 12
TOK_DEV = 1024
BLOCK = 128
GROUP = 8192
TOKENS = 32768
N_DP = 4


def draw_seg_starts(key, part):
    key = jax.random.fold_in(key, 11)
    first_key, last_key = jax.random.split(key, 2)
    opening = jax.random.randint(first_key, (N_DP, 1), 1, TOK_DEV)
    closing = GROUP - TOK_DEV + jax.random.randint(last_key, (N_DP, 1), 1, TOK_DEV)
    place = jnp.arange(GROUP, dtype=jnp.int32)[None, :]
    before_rows = (place < opening) & ((opening - place) % 512 == 0)
    after_rows = (place > closing) & ((place - closing) % 512 == 0)
    starts = (place == 0) | (place == opening) | (place == closing) | before_rows | after_rows
    return starts.astype(jnp.int32).reshape(TOKENS)


def draw_decay_param(key, part):
    key = jax.random.fold_in(key, 23)
    pick_key, slow_key, quick_key = jax.random.split(key, 3)
    quick_mask = jax.random.randint(pick_key, (LRU,), 0, 2) == 0
    slow_rate = jnp.exp(jax.random.uniform(slow_key, (LRU,), jnp.float32, math.log(0.02 / GROUP), math.log(0.3 / GROUP)))
    quick_rate = jnp.exp(jax.random.uniform(quick_key, (LRU,), jnp.float32, math.log(0.005), math.log(0.01)))
    chosen = jnp.where(quick_mask, quick_rate, slow_rate)
    return (-jnp.log(jnp.expm1(chosen))).astype(jnp.bfloat16)


def levels(rng, shape, shards, smallest, top_value):
    def one(axis_at, parts):
        steps = jax.random.uniform(jax.random.fold_in(jax.random.fold_in(rng, 6), axis_at), (parts,), jnp.float32, smallest / len(shards), top_value / len(shards))
        return jnp.repeat(jnp.exp(steps), shape[axis_at] // parts).reshape((-1,) + (1,) * (len(shape) - axis_at - 1))

    gain = one(*shards[0])
    for cut in shards[1:]:
        gain = gain * one(*cut)
    return gain


def scatter_about(own_key, dims, deviation, limit, cuts=(), held_as=jnp.bfloat16):
    factor_of = levels(own_key, dims, cuts, -0.22, 0.18) if cuts else 1.0
    values = jax.random.normal(own_key, dims, jnp.float32) * deviation * factor_of
    return jnp.minimum(jnp.maximum(values, -limit), limit).astype(held_as)


def setup_inputs(seed: int = 0) -> dict:
    splits = jax.random.split(jax.random.key(seed), 19)
    return {
        "tokens": scatter_about(splits[0], (TOKENS, D), 1.0, 6.0, ((0, 32),)),
        "seg_starts": draw_seg_starts(jax.random.fold_in(splits[18], 71), 0),
        "cotangent": scatter_about(splits[2], (TOKENS, D), 1.0, 6.0, ((0, 32),)),
        "recur_in": scatter_about(splits[3], (D, LRU), D ** -0.5, 0.1875, ((0, 32),)),
        "gelu_branch": scatter_about(splits[4], (D, LRU), D ** -0.5, 0.1875, ((0, 32),)),
        "mixer_out": scatter_about(splits[5], (LRU, D), (LRU // 16) ** -0.5, 0.625, ((0, 32),)),
        "conv_weight": scatter_about(splits[6], (CONV, LRU), CONV ** -0.5, 3.0, ((1, 32),)),
        "conv_bias": scatter_about(splits[7], (LRU,), 0.5, 3.0, ((0, 32),)),
        "rate_gate": scatter_about(splits[8], (LRU, BLOCK), BLOCK ** -0.5, 0.5, ((0, 32),)),
        "input_gate": scatter_about(splits[9], (LRU, BLOCK), BLOCK ** -0.5, 0.5, ((0, 32),)),
        "rate_bias": scatter_about(splits[10], (LRU,), 1.0, 4.0, ((0, 32),)),
        "input_bias": scatter_about(splits[11], (LRU,), 1.0, 4.0, ((0, 32),)),
        "decay_param": draw_decay_param(jax.random.fold_in(splits[18], 71), 0),
        "mixer_gain": jnp.clip(0.5 + 1.0 * jax.random.uniform(splits[13], (D,), jnp.float32) ** levels(splits[13], (D,), ((0, 32),), -0.2, 0.2), 0.5, 1.5).astype(jnp.bfloat16),
        "mlp_gate": scatter_about(splits[14], (D, FF), D ** -0.5, 0.1875, ((0, 32),)),
        "mlp_up": scatter_about(splits[15], (D, FF), D ** -0.5, 0.1875, ((0, 32),)),
        "mlp_down": scatter_about(splits[16], (FF, D), (FF // 4) ** -0.5, 0.21875, ((0, 32),)),
        "mlp_gain": jnp.clip(0.5 + 1.0 * jax.random.uniform(splits[17], (D,), jnp.float32) ** levels(splits[17], (D,), ((0, 32),), -0.2, 0.2), 0.5, 1.5).astype(jnp.bfloat16),
    }


EPSILON = 1e-06
RATE_SCALE = 8.0

@jax.custom_vjp
def low(v):
    return lax.optimization_barrier(v.astype(jnp.bfloat16)).astype(jnp.float32)

@jax.custom_vjp
def low_back(v):
    return v

def low_keep(v):
    return (low(v), None)

def low_pass(kept, grad):
    return (grad,)

def back_keep(v):
    return (v, None)

def back_low(kept, grad):
    return (low(grad),)
low.defvjp(low_keep, low_pass)
low_back.defvjp(back_keep, back_low)

def matmul(left_side, right_side):
    return jnp.dot(left_side, right_side, preferred_element_type=jnp.float32, precision=lax.Precision.HIGHEST)

def lagged(values, step_count):
    if step_count == 0:
        return values
    padding = jnp.zeros((step_count,) + values.shape[1:], values.dtype)
    return jnp.concatenate([padding, values[:values.shape[0] - step_count]], axis=0)

def block_product(values, blocks):
    split_vals = values.reshape(values.shape[0], HEADS, BLOCK)
    matrices = blocks.reshape(HEADS, BLOCK, BLOCK)
    result = jnp.einsum('thc,hcd->thd', split_vals, matrices, precision=lax.Precision.HIGHEST)
    return result.reshape(values.shape[0], LRU)

def rms_scale(values):
    return lax.rsqrt(lax.optimization_barrier(jnp.mean(values * values, axis=-1, keepdims=True)) + EPSILON)

def step_state(current, factors):
    current = factors[0] * current + factors[1]
    return (current, current)

def group_forward(inputs, start_flags, weights):
    recur_in, gelu_branch, mixer_out, conv_weight, conv_bias, rate_gate, input_gate, rate_bias, input_bias, decay_param, mixer_gain, mlp_gate, mlp_up, mlp_down, mlp_gain = weights
    norm_one = low(inputs * rms_scale(inputs) * mixer_gain)
    recur_vals = low(low_back(matmul(norm_one, recur_in)))
    branch_act = jax.nn.gelu(low_back(matmul(norm_one, gelu_branch)))
    conv_sum = conv_bias + conv_weight[0] * recur_vals
    validity = jnp.ones_like(start_flags)
    for offset in range(1, CONV):
        validity = validity * (1.0 - lagged(start_flags, offset - 1))
        conv_sum = conv_sum + conv_weight[offset] * validity[:, None] * lagged(recur_vals, offset)
    conv_vals = low(conv_sum)
    rate_act = jax.nn.sigmoid(low_back(block_product(conv_vals, rate_gate)) + rate_bias)
    input_act = jax.nn.sigmoid(low_back(block_product(conv_vals, input_gate)) + input_bias)
    log_decay = -RATE_SCALE * rate_act * jax.nn.softplus(-decay_param)
    decay_now = jnp.exp(log_decay)
    multiplier = jnp.where(start_flags[:, None] > 0.5, 1.0, jnp.sqrt(-jnp.expm1(2.0 * log_decay)))
    carried = decay_now * (1.0 - start_flags)[:, None]
    drive_term = multiplier * input_act * conv_vals
    final_state, states = lax.scan(step_state, jnp.zeros_like(drive_term[0]), (carried, drive_term))
    mixed_vals = low(states * branch_act)
    after_mixer = inputs + low_back(matmul(mixed_vals, mixer_out))
    norm_two = low(after_mixer * rms_scale(after_mixer) * mlp_gain)
    gate_pre = low_back(matmul(norm_two, mlp_gate))
    up_pre = low_back(matmul(norm_two, mlp_up))
    hidden = low(jax.nn.gelu(gate_pre) * up_pre)
    return after_mixer + low_back(matmul(hidden, mlp_down))

def reference(tokens, seg_starts, cotangent, recur_in, gelu_branch, mixer_out, conv_weight, conv_bias, rate_gate, input_gate, rate_bias, input_bias, decay_param, mixer_gain, mlp_gate, mlp_up, mlp_down, mlp_gain):
    weights = tuple((element.astype(jnp.float32) for element in (recur_in, gelu_branch, mixer_out, conv_weight, conv_bias, rate_gate, input_gate, rate_bias, input_bias, decay_param, mixer_gain, mlp_gate, mlp_up, mlp_down, mlp_gain)))
    inputs = tokens.astype(jnp.float32).reshape(N_DP, GROUP, D)
    flag_rows = seg_starts.astype(jnp.float32).reshape(N_DP, GROUP)
    cot_rows = cotangent.astype(jnp.float32).reshape(N_DP, GROUP, D)

    def forward(all_inputs, all_weights):

        def one_group(group_pair):
            return group_forward(group_pair[0], group_pair[1], all_weights)
        return lax.map(jax.checkpoint(one_group), (all_inputs, flag_rows))
    outputs, pull_back = jax.vjp(forward, inputs, weights)
    input_grad, weight_grads = pull_back(cot_rows)
    return (outputs.reshape(TOKENS, D).astype(jnp.bfloat16), input_grad.reshape(TOKENS, D).astype(jnp.bfloat16), weight_grads[0], weight_grads[1], weight_grads[2], weight_grads[3], weight_grads[4], weight_grads[5], weight_grads[6], weight_grads[7], weight_grads[8], weight_grads[9], weight_grads[10], weight_grads[11], weight_grads[12], weight_grads[13], weight_grads[14])
```

```python
import functools

import jax
import jax.numpy as jnp
from jax import lax
from jax.experimental import pallas as pl
from jax.experimental.pallas import tpu as pltpu
from jax.sharding import PartitionSpec as P

AXES = ("dp", "seq")
CONV = 4
EPSILON = 1e-06
RATE_SCALE = 8.0
SUB = 8
CB = 256
HEAD = 128
LEAD = 32
STEP = 128
WIDE = 512
TALL = 512
FB = 768
VMEM = 60 * 1024 * 1024
GROUPS = 32
GELU_C = 0.7978845608028654
GELU_K = 0.044715
F32 = jnp.float32
BF16 = jnp.bfloat16


def params(**extra):
    return pltpu.CompilerParams(vmem_limit_bytes=VMEM, **extra)


def cost(time):
    return pl.CostEstimate(flops=int(time * 1e6), bytes_accessed=0, transcendentals=0)


def once(shape, index_map):
    return pl.BlockSpec(shape, index_map, pipeline_mode=pl.Buffered(1))


def dot(left, right):
    return jnp.dot(left, right, preferred_element_type=F32)


def dot_t(left, right):
    return lax.dot_general(left, right, (((1,), (1,)), ((), ())), preferred_element_type=F32)


def t_dot(left, right):
    return lax.dot_general(left, right, (((0,), (0,)), ((), ())), preferred_element_type=F32)


def staged():
    return lax.axis_size("dp") == 4 and lax.axis_size("dp") * lax.axis_size("seq") == GROUPS


def parity():
    return lax.axis_index("seq") % 2 if staged() else 0


def halves(core, value, pairs):
    value = value.astype(BF16).reshape(pairs, 2, value.shape[0] // (2 * pairs), value.shape[-1])
    zero, one = value[:, 0], value[:, 1]
    return jnp.where(core == 0, zero, one), jnp.where(core == 0, one, zero)


def split(core, value, mine_ref, other_ref, rows):
    mine_ref[:, rows, :], other_ref[:, rows, :] = halves(core, value, mine_ref.shape[0])


def gelu_parts(v):
    square = v * v
    tanh = jnp.tanh(v * (GELU_C + (GELU_C * GELU_K) * square))
    half = 0.5 + 0.5 * tanh
    slope = half + (0.5 * v) * (1.0 - tanh * tanh) * (GELU_C + (3.0 * GELU_C * GELU_K) * square)
    return v * half, slope


def gelu_value(v):
    tanh = jnp.tanh(v * (GELU_C + (GELU_C * GELU_K) * (v * v)))
    return v * (0.5 + 0.5 * tanh)


def decay_parts(rate, neg_soft, flag):
    log_decay = rate * neg_soft
    decay = jnp.exp(log_decay)
    y = 2.0 * log_decay
    series = 1.0 / 720.0
    for k in (120.0, 24.0, 6.0, 2.0, 1.0):
        series = 1.0 / k + y * series
    gap = jnp.where(y > -0.3, -y * series, 1.0 - decay * decay)
    inverse = lax.rsqrt(jnp.maximum(gap, 1e-30))
    return decay, inverse, jnp.where(flag > 0.5, 1.0, gap * inverse)


def sigmoid(v):
    return 0.5 + 0.5 * jnp.tanh(0.5 * v)


def gates(conv_low, gate_ref, small_ref):
    one = dot(conv_low[:, :HEAD], gate_ref[:HEAD, :])
    two = dot(conv_low[:, HEAD:], gate_ref[HEAD:, :])
    rate = sigmoid(
        jnp.concatenate([one[:, :HEAD], two[:, :HEAD]], axis=1) + small_ref[5:6, :]
    )
    enter = sigmoid(
        jnp.concatenate([one[:, HEAD:], two[:, HEAD:]], axis=1) + small_ref[6:7, :]
    )
    return rate, enter


def front_kernel(
    x_ref, xh_ref, gain_ref, w_ref, g_ref, small_ref, mask_ref,
    n1_ref, xb_ref, xc_ref, ab_ref, drive_ref, tot_ref, n1h_ref,
    e_ref,
):
    rows = x_ref.shape[0]

    @pl.when(pl.program_id(0) == 0)
    def _():
        gain = gain_ref[0:1, :]

        def norm(i, carry):
            at = pl.ds(pl.multiple_of(i * STEP, STEP), STEP)
            x = x_ref[at, :].astype(F32)
            scale = lax.rsqrt(jnp.mean(x * x, axis=-1, keepdims=True) + EPSILON)
            n1_ref[at, :] = (x * scale * gain).astype(BF16)
            return carry

        lax.fori_loop(0, rows // STEP, norm, 0)
        xh = xh_ref[...].astype(F32)
        scale = lax.rsqrt(jnp.mean(xh * xh, axis=-1, keepdims=True) + EPSILON)
        n1h_ref[...] = (xh * scale * gain).astype(BF16)

    weight = w_ref[...].reshape(n1_ref.shape[1], CB)

    half = rows // 4
    for i in range(4):
        part = dot(n1_ref[i * half : (i + 1) * half, :], weight).astype(BF16).astype(F32)
        e_ref[LEAD + i * half : LEAD + (i + 1) * half, :] = part
    halo = dot(n1h_ref[...], weight).astype(BF16).astype(F32)
    first = lax.broadcasted_iota(jnp.int32, (SUB, CB), 0) == 0
    e_ref[0:SUB, :] = jnp.zeros((SUB, CB), F32)
    for q in range(1, CONV):
        tile = e_ref[LEAD + rows - SUB * q : LEAD + rows - SUB * (q - 1), :]
        tile = pltpu.roll(tile, 1, 0)
        e_ref[LEAD - SUB * q : LEAD - SUB * (q - 1), :] = jnp.where(
            first, jnp.broadcast_to(halo[q - 1 : q, :], (SUB, CB)), tile
        )
    xb_ref[...] = e_ref[...].astype(BF16)

    def chunk(i, carry):
        base = pl.multiple_of(i * WIDE, WIDE)
        at = pl.ds(base, WIDE)
        mask = mask_ref[at, :]
        total = small_ref[4:5, :] + small_ref[0:1, :] * e_ref[pl.ds(base + LEAD, WIDE), :]
        for k in range(1, CONV):
            shifted = e_ref[pl.ds(base + LEAD - SUB * k, WIDE), :]
            total = total + (small_ref[k : k + 1, :] * mask[:, k : k + 1]) * shifted
        low = total.astype(BF16)
        xc_ref[at, :] = low
        rate, enter = gates(low, g_ref, small_ref)
        flag = mask[:, 0:1]
        decay, _, multiplier = decay_parts(rate, small_ref[7:8, :], flag)
        drive = multiplier * enter * low.astype(F32)
        abar = decay * (1.0 - flag)
        ab_ref[at, :] = abar
        drive_ref[at, :] = drive
        product, state = carry
        for t in range(WIDE // SUB):
            a = abar[t * SUB : (t + 1) * SUB, :]
            product = product * a
            state = state * a + drive[t * SUB : (t + 1) * SUB, :]
        return product, state

    start = (jnp.ones((SUB, CB), F32), jnp.zeros((SUB, CB), F32))
    product, state = lax.fori_loop(0, rows // WIDE, chunk, start)
    tot_ref[0:SUB, :] = product
    tot_ref[SUB : 2 * SUB, :] = state
    whole_p, whole_s = product[0:1, :], state[0:1, :]
    for s in range(1, SUB):
        whole_s = whole_s * product[s : s + 1, :] + state[s : s + 1, :]
        whole_p = whole_p * product[s : s + 1, :]
    tot_ref[2 * SUB : 2 * SUB + 1, :] = whole_p
    tot_ref[2 * SUB + 1 : 2 * SUB + 2, :] = whole_s
    tot_ref[2 * SUB + 2 : 3 * SUB, :] = jnp.zeros((SUB - 2, CB), F32)


def front(x, x_halo, gain, recur_blocks, gate_pair, small, mask):
    rows, width = x.shape
    lru = gate_pair.shape[0]
    devices, per = recur_blocks.shape[0], width // recur_blocks.shape[0]
    col = lambda r: pl.BlockSpec((r, CB), lambda j: (0, j))
    return pl.pallas_call(
        front_kernel,
        grid=(lru // CB,),
        in_specs=[
            once((rows, width), lambda j: (0, 0)),
            once(x_halo.shape, lambda j: (0, 0)),
            once((1, width), lambda j: (0, 0)),
            pl.BlockSpec((devices, per, CB), lambda j: (0, j, 0)),
            pl.BlockSpec((CB, 2 * HEAD), lambda j: (j, 0)),
            col(SUB),
            once(mask.shape, lambda j: (0, 0)),
        ],
        out_specs=[
            once((rows, width), lambda j: (0, 0)),
            col(rows + LEAD), col(rows), col(rows), col(rows), col(3 * SUB),
            once(x_halo.shape, lambda j: (0, 0)),
        ],
        out_shape=[
            jax.ShapeDtypeStruct((rows, width), BF16),
            jax.ShapeDtypeStruct((rows + LEAD, lru), BF16),
            jax.ShapeDtypeStruct((rows, lru), BF16),
            jax.ShapeDtypeStruct((rows, lru), F32),
            jax.ShapeDtypeStruct((rows, lru), F32),
            jax.ShapeDtypeStruct((3 * SUB, lru), F32),
            jax.ShapeDtypeStruct(x_halo.shape, BF16),
        ],
        scratch_shapes=[pltpu.VMEM((rows + LEAD, CB), F32)],
        compiler_params=params(),
        cost_estimate=cost(33),
        name="front",
    )(x, x_halo, gain, recur_blocks, gate_pair, small, mask)


def branch_kernel(n_ref, w_ref, out_ref):
    out_ref[...] = dot(n_ref[...], w_ref[...].reshape(n_ref.shape[1], CB)).astype(BF16)


def branch(n1, bundle, lru):
    rows, width = n1.shape
    devices, steps = bundle.shape[0], lru // CB
    own = width // devices
    return pl.pallas_call(
        branch_kernel,
        grid=(lru // CB,),
        in_specs=[
            once((rows, width), lambda j: (0, 0)),
            pl.BlockSpec((devices, own, CB), lambda j: (0, j, 0)),
        ],
        out_specs=pl.BlockSpec((rows, CB), lambda j: (0, j)),
        out_shape=jax.ShapeDtypeStruct((rows, lru), BF16),
        compiler_params=params(),
        cost_estimate=cost(8),
        name="branch",
    )(n1, bundle)


def mix_kernel(*refs, pieces):
    ab_ref, drive_ref, yp_ref, x_ref, w0_ref, w1_ref, w2_ref, w3_ref, tot_ref, gain_ref = refs[:10]
    piece_refs = refs[10 : 10 + pieces]
    h_ref, z_ref, x1_ref, n2_ref, ent_ref, state_ref, piece_ref = refs[-7:]
    rows = ab_ref.shape[0]

    @pl.when(pl.program_id(0) == 0)
    def _():
        for k, ref in enumerate(piece_refs):
            piece_ref[k * SUB : (k + 1) * SUB, :] = ref[...]
        enter = fold_before(piece_ref)
        for s in range(SUB):
            ent_ref[s : s + 1, :] = enter
            enter = tot_ref[s : s + 1, :] * enter + tot_ref[SUB + s : SUB + s + 1, :]
        state_ref[...] = ent_ref[...]

    def tiles(i, state):
        at = pl.ds(pl.multiple_of(i * 2 * SUB, 2 * SUB), 2 * SUB)
        a, d = ab_ref[at, :], drive_ref[at, :]
        one = a[:SUB, :] * state + d[:SUB, :]
        two = a[SUB:, :] * one + d[SUB:, :]
        h = jnp.concatenate([one, two], axis=0)
        h_ref[at, :] = h.astype(BF16)
        z_ref[at, :] = (h * gelu_value(yp_ref[at, :].astype(F32))).astype(BF16)
        return two

    state_ref[...] = lax.fori_loop(0, rows // (2 * SUB), tiles, state_ref[...])
    z = z_ref[...]
    mixed = [dot(z, w[...].reshape(z.shape[1], CB)) for w in (w0_ref, w1_ref, w2_ref, w3_ref)]
    x1 = x_ref[...].astype(F32) + jnp.concatenate(mixed, axis=1)
    x1_ref[...] = x1
    scale = lax.rsqrt(jnp.mean(x1 * x1, axis=-1, keepdims=True) + EPSILON)
    n2_ref[...] = (x1 * scale * gain_ref[0:1, :]).astype(BF16)


def out_blocks(bundle, lru, width):
    devices = bundle.shape[0]
    own, ahead = lru // devices, (lru // CB) * (width // devices) // (lru // devices)
    return [
        once((devices, own, CB), lambda i, c=c: (0, ahead + c, 0)) for c in range(width // CB)
    ]


def mix(abar, drive, yp, x, bundle, tot, pieces, gain):
    rows, lru = abar.shape
    width = x.shape[1]
    weights = out_blocks(bundle, lru, width)
    block = 256
    row = lambda w: pl.BlockSpec((block, w), lambda i: (i, 0))
    whole = lambda a: once(a.shape, lambda i: (0, 0))
    return pl.pallas_call(
        functools.partial(mix_kernel, pieces=len(pieces)),
        grid=(rows // block,),
        in_specs=[
            row(lru), row(lru), row(lru), row(width),
            *weights, whole(tot), whole(gain), *[whole(piece) for piece in pieces],
        ],
        out_specs=[row(lru), row(lru), row(width), row(width), pl.BlockSpec((SUB, lru), lambda i: (0, 0))],
        out_shape=[
            jax.ShapeDtypeStruct((rows, lru), BF16),
            jax.ShapeDtypeStruct((rows, lru), BF16),
            jax.ShapeDtypeStruct((rows, width), F32),
            jax.ShapeDtypeStruct((rows, width), BF16),
            jax.ShapeDtypeStruct((SUB, lru), F32),
        ],
        scratch_shapes=[
            pltpu.VMEM((SUB, lru), F32), pltpu.VMEM((SUB * len(pieces), lru), F32),
        ],
        compiler_params=params(),
        cost_estimate=cost(15),
        name="mix",
    )(abar, drive, yp, x, *[bundle] * len(weights), tot, gain, *pieces)


def mlp_kernel(*refs, begins, ends):
    n_ref, g_ref, gate_ref, up_ref, d0_ref, d1_ref, d2_ref, d3_ref = refs[:8]
    refs = refs[8:]
    if not begins:
        acc_in_ref, dx_in_ref, _, _ = refs[:4]
        refs = refs[4:]
    if ends:
        x1_hbm, gain_ref, out_ref, dx_ref, do_ref, gg_ref = refs[:6]
        refs = refs[6:]
    else:
        acc_ref, dx_ref = refs[:2]
        refs = refs[2:]
    gu_mine_ref, gu_other_ref, down_mine_ref, down_other_ref = refs[:4]
    nt_ref, mm_ref, dl_ref, wt_ref, dt_ref = refs[4:9]
    if ends:
        acc_ref, x1_ref, x1_sem = refs[9:12]
    rows, width = n_ref.shape
    step = TALL
    j = pl.program_id(0)

    @pl.when(j == 0)
    def _():
        nt_ref[...] = n_ref[...].T
        if begins:
            acc_ref[...] = jnp.zeros_like(acc_ref)
            dx_ref[...] = jnp.zeros_like(dx_ref)
        else:
            acc_ref[...] = acc_in_ref[...]
            dx_ref[...] = dx_in_ref[...]

    own = gate_ref.shape[1] * CB // FB
    for p in range(FB // CB):
        here = slice(p * own, (p + 1) * own)
        wt_ref[:, p * CB : (p + 1) * CB] = gate_ref[:, here, :].reshape(width, CB)
        wt_ref[:, FB + p * CB : FB + (p + 1) * CB] = up_ref[:, here, :].reshape(width, CB)
    for c, ref in enumerate((d0_ref, d1_ref, d2_ref, d3_ref)):
        dt_ref[:, c * CB : (c + 1) * CB] = ref[...].reshape(FB, CB)

    def part(i, carry):
        at = pl.ds(pl.multiple_of(i * step, step), step)
        n, g = n_ref[at, :], g_ref[at, :]
        both = dot(n, wt_ref[...])
        gate_act, slope = gelu_parts(both[:, :FB])
        up = both[:, FB:]
        mm = (gate_act * up).astype(BF16)
        mm_ref[at, :] = mm
        grad = dot_t(g, dt_ref[...])
        dl_ref[at, :FB] = (grad * up * slope).astype(BF16)
        dl_ref[at, FB:] = (grad * gate_act).astype(BF16)
        acc_ref[at, :] += dot(mm, dt_ref[...])
        dx_ref[at, :] += dot_t(dl_ref[at, :], wt_ref[...])
        return carry

    lax.fori_loop(0, rows // step, part, 0, unroll=True)
    core = parity()
    per = gu_mine_ref.shape[1] // 2
    split(core, dot(nt_ref[...], dl_ref[:, :FB]), gu_mine_ref, gu_other_ref, slice(0, per))
    split(core, dot(nt_ref[...], dl_ref[:, FB:]), gu_mine_ref, gu_other_ref, slice(per, 2 * per))
    downs = halves(core, t_dot(mm_ref[...], g_ref[...]), down_mine_ref.shape[0])
    for owned, ref in zip(downs, (down_mine_ref, down_other_ref)):
        rows_own = owned.shape[1]
        ref[:, :rows_own, :] = owned[:, :, :FB]
        third = rows_own // 3
        for p in range(3):
            ref[:, rows_own:, p * CB : (p + 1) * CB] = owned[:, p * third : (p + 1) * third, FB:]

    if ends:

        @pl.when(j == pl.num_programs(0) - 1)
        def _():
            gain = gain_ref[0:1, :]

            def fetch(i):
                at = pl.ds(pl.multiple_of(i * STEP, STEP), STEP)
                slot = lax.rem(i, 2)
                return pltpu.make_async_copy(x1_hbm.at[at], x1_ref.at[slot], x1_sem.at[slot])

            fetch(0).start()

            def close(i, total):
                at = pl.ds(pl.multiple_of(i * STEP, STEP), STEP)

                @pl.when(i + 1 < rows // STEP)
                def _():
                    fetch(i + 1).start()

                fetch(i).wait()
                x1 = x1_ref[lax.rem(i, 2)]
                out_ref[at, :] = (x1 + acc_ref[at, :]).astype(BF16)
                scale = lax.rsqrt(jnp.mean(x1 * x1, axis=-1, keepdims=True) + EPSILON)
                q = x1 * scale
                dn = dx_ref[at, :]
                w = dn * gain
                inner = jnp.mean(w * q, axis=-1, keepdims=True)
                dx = g_ref[at, :].astype(F32) + scale * (w - q * inner)
                dx_ref[at, :] = dx
                do_ref[at, :] = dx.astype(BF16)
                return total + jnp.sum(dn * q, axis=0, keepdims=True)

            gg_ref[...] = jnp.broadcast_to(
                lax.fori_loop(0, rows // STEP, close, jnp.zeros((1, width), F32)), gg_ref.shape
            )


def mlp(n2, g, bundle, hidden, start, count, before=None, close=None):
    rows, width = n2.shape
    devices, steps = bundle.shape[0], hidden // FB
    own, per = width // devices, hidden // devices
    group = FB // per
    whole = lambda s: once(s, lambda j: (0, 0))
    lines = own * (FB // CB)
    gate = pl.BlockSpec((devices, lines, CB), lambda j: (0, start + j, 0))
    up = pl.BlockSpec((devices, lines, CB), lambda j: (0, steps + start + j, 0))
    downs = [
        pl.BlockSpec((group, per, CB), lambda j, c=c: (start + j, 2 * steps * lines // per + c, 0))
        for c in range(width // CB)
    ]
    pair = pl.BlockSpec((devices // 2, 2 * own, FB), lambda j: (0, j, 0))
    lines_down = per * width // FB
    half = pl.BlockSpec((group // 2, lines_down, FB), lambda j: (start + j, 0, 0))
    operands = [n2, g, bundle, bundle, *[bundle] * len(downs)]
    in_specs = [whole(n2.shape), whole(g.shape), gate, up, *downs]
    shape_f = jax.ShapeDtypeStruct((rows, width), F32)
    shape_b = jax.ShapeDtypeStruct((rows, width), BF16)
    aliases = {}
    if before is not None:
        operands += before
        in_specs += [whole(shape_f.shape)] * 2 + [pl.BlockSpec(memory_space=pl.ANY)] * 2
    if close is not None:
        operands += close
        in_specs += [pl.BlockSpec(memory_space=pl.ANY), whole(close[1].shape)]
        outs = [shape_b, shape_f, shape_b, jax.ShapeDtypeStruct((SUB, width), F32)]
    else:
        outs = [shape_f, shape_f]
    out_specs = [whole(shape.shape) for shape in outs]
    if before is not None:
        aliases = {10: len(outs) + 2, 11: len(outs) + 3}
    gu = jax.ShapeDtypeStruct((devices // 2, 2 * own * count, FB), BF16)
    down = jax.ShapeDtypeStruct((devices // 2, lines_down, FB), BF16)
    return pl.pallas_call(
        functools.partial(mlp_kernel, begins=before is None, ends=close is not None),
        grid=(count,),
        in_specs=in_specs,
        out_specs=out_specs + [pair, pair, half, half],
        out_shape=outs + [gu, gu, down, down],
        scratch_shapes=[
            pltpu.VMEM((width, rows), BF16),
            pltpu.VMEM((rows, FB), BF16),
            pltpu.VMEM((rows, 2 * FB), BF16),
            pltpu.VMEM((width, 2 * FB), BF16),
            pltpu.VMEM((FB, width), BF16),
        ]
        + (
            [
                pltpu.VMEM((rows, width), F32),
                pltpu.VMEM((2, STEP, width), F32),
                pltpu.SemaphoreType.DMA((2,)),
            ]
            if close is not None
            else []
        ),
        input_output_aliases=aliases,
        compiler_params=params(),
        cost_estimate=cost(20 * count),
        name="mlp",
    )(*operands)


def turn_kernel(
    do_ref, w0_ref, w1_ref, w2_ref, w3_ref, yp_ref, h_ref, ab_ref, tot_ref,
    dh_ref, dyp_ref, back_ref,
    dz_ref, w_ref,
):
    rows, width = do_ref.shape

    @pl.when(pl.program_id(0) == 0)
    def _():
        for c, ref in enumerate((w0_ref, w1_ref, w2_ref, w3_ref)):
            w_ref[:, c * CB : (c + 1) * CB] = ref[...].reshape(w_ref.shape[0], CB)

    weight = w_ref[pl.ds(pl.multiple_of(pl.program_id(0) * CB, CB), CB), :]
    half = rows // 4
    for i in range(4):
        dz_ref[i * half : (i + 1) * half, :] = dot_t(do_ref[i * half : (i + 1) * half, :], weight)

    def chunk(i, carry):
        base = pl.multiple_of((rows // WIDE - 1 - i) * WIDE, WIDE)
        at = pl.ds(base, WIDE)
        dz = dz_ref[at, :]
        act, slope = gelu_parts(yp_ref[at, :].astype(F32))
        dh = dz * act
        dh_ref[at, :] = dh
        dyp_ref[at, :] = (dz * h_ref[at, :].astype(F32) * slope).astype(BF16)
        abar = ab_ref[at, :]
        leave = carry
        for t in reversed(range(WIDE // SUB)):
            here = slice(t * SUB, (t + 1) * SUB)
            leave = abar[here, :] * (dh[here, :] + leave)
        return leave

    leave = lax.fori_loop(0, rows // WIDE, chunk, jnp.zeros((SUB, CB), F32))
    back_ref[0:SUB, :] = leave
    whole = leave[SUB - 1 : SUB, :]
    for s in reversed(range(SUB - 1)):
        whole = whole * tot_ref[s : s + 1, :] + leave[s : s + 1, :]
    back_ref[SUB : SUB + 1, :] = tot_ref[2 * SUB : 2 * SUB + 1, :]
    back_ref[SUB + 1 : SUB + 2, :] = whole
    back_ref[SUB + 2 : 2 * SUB, :] = jnp.zeros((SUB - 2, CB), F32)


def turn(do1, bundle, yp, h, abar, tot):
    rows, width = do1.shape
    lru = abar.shape[1]
    weights = out_blocks(bundle, lru, width)
    col = lambda r: pl.BlockSpec((r, CB), lambda j: (0, j))
    return pl.pallas_call(
        turn_kernel,
        grid=(lru // CB,),
        in_specs=[
            once((rows, width), lambda j: (0, 0)),
            *weights,
            col(rows), col(rows), col(rows), col(3 * SUB),
        ],
        out_specs=[col(rows), col(rows), col(2 * SUB)],
        out_shape=[
            jax.ShapeDtypeStruct((rows, lru), F32),
            jax.ShapeDtypeStruct((rows, lru), BF16),
            jax.ShapeDtypeStruct((2 * SUB, lru), F32),
        ],
        scratch_shapes=[pltpu.VMEM((rows, CB), F32), pltpu.VMEM((lru, width), BF16)],
        compiler_params=params(),
        cost_estimate=cost(15),
        name="turn",
    )(do1, *[bundle] * len(weights), yp, h, abar, tot)


def side_kernel(
    n_ref, dyp_ref, w_ref, z_ref, do_ref,
    both_ref, dn_ref,
    nt_ref,
):
    @pl.when(pl.program_id(0) == 0)
    def _():
        nt_ref[...] = n_ref[...].T
        dn_ref[...] = jnp.zeros_like(dn_ref)

    j = pl.program_id(0)
    width, block = n_ref.shape[1], dyp_ref.shape[1]
    own = w_ref.shape[1] * CB // block
    columns = pl.ds(pl.multiple_of(j * block, block), block)
    devices = both_ref.shape[0]
    both_ref[:, :own, columns] = dot(nt_ref[...], dyp_ref[...]).astype(BF16).reshape(devices, own, block)
    for p in range(block // CB):
        weight = w_ref[:, p * own : (p + 1) * own, :].reshape(width, CB)
        dn_ref[...] += dot_t(dyp_ref[:, p * CB : (p + 1) * CB], weight)
    half = devices // 2
    there = pl.ds(pl.multiple_of(j * half, half), half)
    out = t_dot(z_ref[...], do_ref[...]).astype(BF16).reshape(half, block // half, width)
    both_ref[there, own : 2 * own, :width] = out[:, :own, :]
    both_ref[there, own : own + own // 2, width:] = out[:, own:, : width // 2]
    both_ref[there, own + own // 2 : 2 * own, width:] = out[:, own:, width // 2 :]


def side(n1, dyp, weight, z, do1, devices):
    rows, width = n1.shape
    lru = dyp.shape[1]
    block = lru // 2
    both = (devices, 2 * (width // devices), lru)
    whole = once((rows, width), lambda j: (0, 0))
    col = pl.BlockSpec((rows, block), lambda j: (0, j))
    return pl.pallas_call(
        side_kernel,
        grid=(lru // block,),
        in_specs=[
            whole, col,
            pl.BlockSpec((devices, block // CB * (width // devices), CB), lambda j: (0, j, 0)),
            col, whole,
        ],
        out_specs=[once(both, lambda j: (0, 0, 0)), whole],
        out_shape=[
            jax.ShapeDtypeStruct(both, BF16),
            jax.ShapeDtypeStruct((rows, width), F32),
        ],
        scratch_shapes=[pltpu.VMEM((width, rows), BF16)],
        compiler_params=params(),
        cost_estimate=cost(16),
        name="side",
    )(n1, dyp, weight, z, do1)


def rear_kernel(*refs, pieces):
    dh_ref, xc_ref, ab_ref, h_ref, ent_ref, xb_ref, g_ref, small_ref, mask_ref, back_ref, tot_ref = refs[:11]
    piece_refs = refs[11 : 11 + pieces]
    dxb_ref, dg_ref, sum_ref, ret_ref, cin_ref, dxc_ref, dl_ref, piece_ref = refs[-8:]
    rows = dh_ref.shape[0]
    for k, ref in enumerate(piece_refs):
        piece_ref[k * SUB : (k + 1) * SUB, :] = ref[...]
    neg_soft = small_ref[7:8, :]

    leave = fold_after(piece_ref)
    for s in reversed(range(SUB)):
        cin_ref[s : s + 1, :] = leave
        leave = tot_ref[s : s + 1, :] * leave + back_ref[s : s + 1, :]

    def chunk(i, carry):
        leave, sums = carry
        base = pl.multiple_of((rows // rows - 1 - i) * rows, rows)
        at = pl.ds(base, rows)
        mask = mask_ref[at, :]
        flag = mask[:, 0:1]
        low = xc_ref[at, :]
        conv = low.astype(F32)
        rate, enter = gates(low, g_ref, small_ref)
        decay, inverse, multiplier = decay_parts(rate, neg_soft, flag)
        abar = ab_ref[at, :]
        dh = dh_ref[at, :]
        parts = []
        for t in reversed(range(rows // SUB)):
            here = slice(t * SUB, (t + 1) * SUB)
            delta = dh[here, :] + leave
            leave = abar[here, :] * delta
            parts.append(delta)
        delta = jnp.concatenate(parts[::-1], axis=0)
        now = h_ref[at, :].astype(F32)
        before_at = pl.ds(pl.multiple_of(jnp.maximum(base - 2 * SUB, 0), 2 * SUB), 2 * SUB)
        before = h_ref[before_at, :].astype(F32)[SUB:, :]
        before = jnp.where(base == 0, ent_ref[...], before)
        prior = jnp.concatenate([before, now[: rows - SUB, :]], axis=0)
        gated = delta * enter
        dla = (1.0 - flag) * decay * (delta * prior - gated * conv * (decay * inverse))
        by_rate = dla * rate
        dr = neg_soft * by_rate * (1.0 - rate)
        scaled = delta * multiplier
        di = scaled * conv * enter * (1.0 - enter)
        drl, dil = dr.astype(BF16), di.astype(BF16)
        one = jnp.concatenate([drl[:, :HEAD], dil[:, :HEAD]], axis=1)
        two = jnp.concatenate([drl[:, HEAD:], dil[:, HEAD:]], axis=1)
        dl_ref[at, : 2 * HEAD] = one
        dl_ref[at, 2 * HEAD :] = two
        through = jnp.concatenate(
            [dot_t(one, g_ref[:HEAD, :]), dot_t(two, g_ref[HEAD:, :])], axis=1
        )
        dxc = scaled * enter + through
        dxc_ref[at, :] = dxc
        fold = lambda v: functools.reduce(
            lambda a, b: a + b, [v[t * SUB : (t + 1) * SUB, :] for t in range(rows // SUB)]
        )
        new = [fold(dr), fold(di), fold(by_rate), fold(dxc)]
        for k in range(CONV):
            more = 2 * SUB * (k % 2)
            lines = pl.ds(pl.multiple_of(base + LEAD - SUB * (k + k % 2), 2 * SUB), rows + more)
            shift = xb_ref[lines, :].astype(F32)[more // 2 : more // 2 + rows, :]
            term = dxc * shift
            if k:
                term = term * mask[:, k : k + 1]
            new.append(fold(term))
        return leave, tuple(a + b for a, b in zip(sums, new))

    zero = jnp.zeros((SUB, CB), F32)
    _, sums = lax.fori_loop(0, rows // rows, chunk, (cin_ref[...], (zero,) * 8))
    for r, value in enumerate(sums):
        sum_ref[r : r + 1, :] = jnp.sum(value, axis=0, keepdims=True)

    for q in range(CONV - 1):
        tile = dxc_ref[q * SUB : (q + 1) * SUB, :]
        dxc_ref[rows + q * SUB : rows + (q + 1) * SUB, :] = pltpu.roll(tile, SUB - 1, 0)
    for q in range(1, CONV):
        back = jnp.zeros((1, CB), F32)
        for k in range(q, CONV):
            t = (k - q) * SUB
            back = back + small_ref[k : k + 1, :] * mask_ref[t : t + 1, k : k + 1] * dxc_ref[t : t + 1, :]
        ret_ref[q - 1 : q, :] = back
    ret_ref[CONV - 1 :, :] = jnp.zeros((SUB - CONV + 1, CB), F32)

    def spread(i, carry):
        base = pl.multiple_of(i * rows, rows)
        total = small_ref[0:1, :] * dxc_ref[pl.ds(base, rows), :]
        for k in range(1, CONV):
            at = pl.ds(base + SUB * k, rows)
            total = total + (small_ref[k : k + 1, :] * mask_ref[at, k : k + 1]) * dxc_ref[at, :]
        dxb_ref[pl.ds(base, rows), :] = total.astype(BF16)
        return carry

    lax.fori_loop(0, rows // rows, spread, 0)
    dg_ref[:HEAD, :] = t_dot(xc_ref[:, :HEAD], dl_ref[:, : 2 * HEAD])
    dg_ref[HEAD:, :] = t_dot(xc_ref[:, HEAD:], dl_ref[:, 2 * HEAD :])


def rear(dh, xc, abar, h, ent, xb, gate_pair, small, mask, back, tot, pieces, start, count, before=()):
    rows, lru = dh.shape
    col = lambda r: pl.BlockSpec((r, CB), lambda j: (0, start + j))
    pair = pl.BlockSpec((CB, 2 * HEAD), lambda j: (start + j, 0))
    operands = [dh, xc, abar, h, ent, xb, gate_pair, small, mask, back, tot, *pieces, *before]
    return pl.pallas_call(
        functools.partial(rear_kernel, pieces=len(pieces)),
        grid=(count,),
        in_specs=[
            col(rows), col(rows), col(rows), col(rows), col(SUB), col(rows + LEAD), pair, col(SUB),
            once(mask.shape, lambda j: (0, 0)),
            col(2 * SUB), col(3 * SUB),
        ]
        + [col(SUB)] * len(pieces)
        + [pl.BlockSpec(memory_space=pl.ANY)] * len(before),
        out_specs=[col(rows), pair, col(SUB), col(SUB)],
        out_shape=[
            jax.ShapeDtypeStruct((rows, lru), BF16),
            jax.ShapeDtypeStruct((lru, 2 * HEAD), F32),
            jax.ShapeDtypeStruct((SUB, lru), F32),
            jax.ShapeDtypeStruct((SUB, lru), F32),
        ],
        scratch_shapes=[
            pltpu.VMEM((SUB, CB), F32),
            pltpu.VMEM((rows + LEAD, CB), F32),
            pltpu.VMEM((rows, 4 * HEAD), BF16),
            pltpu.VMEM((SUB * len(pieces), CB), F32),
        ],
        input_output_aliases={len(operands) - len(before) + i: i for i in range(len(before))},
        compiler_params=params(),
        cost_estimate=cost(7 * count),
        name="rear",
    )(*operands)


def with_edge(dxb_ref, ret_ref):
    rows, width = dxb_ref.shape
    lastly = lax.broadcasted_iota(jnp.int32, (SUB, width), 0) == SUB - 1
    tail = dxb_ref[rows - 4 * SUB :, :].astype(F32)
    tiles = [tail[:SUB, :]]
    for q in reversed(range(1, CONV)):
        tile = tail[(4 - q) * SUB : (5 - q) * SUB, :]
        tiles.append(tile + jnp.where(lastly, ret_ref[q - 1 : q, :], 0.0))
    return jnp.concatenate(tiles, axis=0).astype(BF16)


def weigh_kernel(n_ref, nh_ref, d_ref, ret_ref, dp_ref, mine_ref, other_ref, nt_ref):
    @pl.when(pl.program_id(0) == 0)
    def _():
        nt_ref[...] = n_ref[...].T

    width = n_ref.shape[1]
    core = parity()
    per = width // (2 * mine_ref.shape[0])
    edge = jnp.concatenate([ret_ref[...], jnp.zeros_like(ret_ref)], axis=0).astype(BF16)
    grad = dot(nt_ref[...], d_ref[...]) + t_dot(nh_ref[...], edge)
    split(core, grad, mine_ref, other_ref, slice(0, per))
    devices, lines, wide = dp_ref.shape
    pair = jnp.concatenate([dp_ref[...], jnp.zeros_like(dp_ref)], axis=1)
    split(core, pair.reshape(devices * 2 * lines, wide), mine_ref, other_ref, slice(per, per + 2 * lines))


def weigh(n1, n1_halo, dxb, ret, dpair):
    rows, width = n1.shape
    lru = dxb.shape[1]
    devices, per = GROUPS, width // GROUPS
    col = lambda r: pl.BlockSpec((r, CB), lambda j: (0, j))
    lines = lru // devices // (lru // CB)
    dpair = dpair.reshape(devices, lru // devices, 2 * HEAD)
    bundle = pl.BlockSpec((devices // 2, per + 2 * lines, CB), lambda j: (0, 0, j))
    shape = jax.ShapeDtypeStruct((devices // 2, per + 2 * lines, lru), BF16)
    return pl.pallas_call(
        weigh_kernel,
        grid=(lru // CB,),
        in_specs=[
            once(n1.shape, lambda j: (0, 0)), once(n1_halo.shape, lambda j: (0, 0)), col(rows), col(SUB),
            pl.BlockSpec((devices, lines, 2 * HEAD), lambda j: (0, j, 0)),
        ],
        out_specs=[bundle, bundle],
        out_shape=[shape, shape],
        scratch_shapes=[pltpu.VMEM((width, rows), BF16)],
        compiler_params=params(),
        cost_estimate=cost(8),
        name="weigh",
    )(n1, n1_halo, dxb, ret, dpair)


def last_kernel(d_ref, ret_ref, w_ref, dn_ref, x_ref, dx_ref, gain_ref, out_ref, wt_ref, e_ref):
    rows, width = x_ref.shape
    block = 256

    @pl.when(pl.program_id(0) == 0)
    def _():
        own = w_ref.shape[1] * CB // wt_ref.shape[1]
        for p in range(wt_ref.shape[1] // CB):
            here = slice(p * own, (p + 1) * own)
            wt_ref[:, p * CB : (p + 1) * CB] = w_ref[:, here, :].reshape(width, CB)

    x = x_ref[...].astype(F32)
    scale = lax.rsqrt(jnp.mean(x * x, axis=-1, keepdims=True) + EPSILON)
    q = x * scale
    e_ref[...] = d_ref[...]

    @pl.when(pl.program_id(0) == pl.num_programs(0) - 1)
    def _():
        e_ref[rows - 4 * SUB :, :] = with_edge(d_ref, ret_ref)

    dn = dn_ref[...] + dot_t(e_ref[...], wt_ref[...])
    w = dn * gain_ref[0:1, :]
    inner = jnp.mean(w * q, axis=-1, keepdims=True)
    out_ref[...] = (dx_ref[...] + scale * (w - q * inner)).astype(BF16)


def last(dxb, ret, recur_blocks, dn, x, dx1, gain):
    rows, lru = dxb.shape
    width = x.shape[1]
    devices, per = recur_blocks.shape[0], width // recur_blocks.shape[0]
    block = 256
    row = lambda w: pl.BlockSpec((block, w), lambda i: (i, 0))
    return pl.pallas_call(
        last_kernel,
        grid=(rows // block,),
        in_specs=[
            row(lru), once(ret.shape, lambda i: (0, 0)),
            once((devices, per * (lru // CB), CB), lambda i: (0, 0, 0)),
            row(width), row(width), row(width), once(gain.shape, lambda i: (0, 0)),
        ],
        out_specs=row(width),
        out_shape=jax.ShapeDtypeStruct(x.shape, BF16),
        scratch_shapes=[pltpu.VMEM((width, lru), BF16), pltpu.VMEM((block, lru), BF16)],
        compiler_params=params(),
        cost_estimate=cost(11),
        name="last",
    )(dxb, ret, recur_blocks, dn, x, dx1, gain)


def interleave(values):
    return values.reshape((SUB, values.shape[0] // SUB) + values.shape[1:]).swapaxes(0, 1).reshape(values.shape)


def uninterleave(values):
    return values.reshape((values.shape[0] // SUB, SUB) + values.shape[1:]).swapaxes(0, 1).reshape(values.shape)


def exchange(value):
    core = lax.axis_index("seq") % 2
    came = permute(value, 0, 1)
    pair = jnp.concatenate(
        [
            jnp.where(core == 0, value, came),
            jnp.where(core == 0, came, value),
            jnp.zeros((SUB - 2 * value.shape[0],) + value.shape[1:], value.dtype),
        ],
        axis=0,
    )
    count = lax.axis_size("seq") // 2
    return [pair] + [permute(pair, 0, 2 * k) for k in range(1, count)]


def fold_before(piece_ref):
    place = lax.axis_index("seq")
    at = place // 2
    value = jnp.zeros((1, piece_ref.shape[1]), F32)
    for k in range(piece_ref.shape[0] // SUB):
        rows = piece_ref[pl.ds(pl.multiple_of((at ^ k) * SUB, SUB), SUB), :]
        value = jnp.where(2 * k < place, rows[0:1, :] * value + rows[1:2, :], value)
        value = jnp.where(2 * k + 1 < place, rows[2:3, :] * value + rows[3:4, :], value)
    return value


def fold_after(piece_ref):
    place = lax.axis_index("seq")
    at = place // 2
    value = jnp.zeros((1, piece_ref.shape[1]), F32)
    for k in reversed(range(piece_ref.shape[0] // SUB)):
        rows = piece_ref[pl.ds(pl.multiple_of((at ^ k) * SUB, SUB), SUB), :]
        value = jnp.where(2 * k + 1 > place, rows[2:3, :] * value + rows[3:4, :], value)
        value = jnp.where(2 * k > place, rows[0:1, :] * value + rows[1:2, :], value)
    return value


def pack_kernel(*refs, layout):
    outs = refs[len(refs) - len({at[0] for at in layout}) :]
    for out, row, source, column in layout:
        block = refs[source][:, column : column + CB]
        outs[out][row : row + block.shape[0], :] = block


def pack(*bundles):
    layout, sources, shapes = [], [], []
    for out, arrays in enumerate(bundles):
        row = 0
        for array in arrays:
            for column in range(0, array.shape[1], CB):
                layout.append((out, row, len(sources), column))
                row += array.shape[0]
            sources.append(array)
        shapes.append(jax.ShapeDtypeStruct((row, CB), BF16))
    return pl.pallas_call(
        functools.partial(pack_kernel, layout=tuple(layout)),
        out_shape=shapes,
        compiler_params=params(),
        cost_estimate=cost(2),
        name="pack",
    )(*sources)


def place_kernel(*refs, slots):
    pieces, out, sems = refs[: len(slots)], refs[len(slots)], refs[len(slots) + 1]
    at_dp, place = lax.axis_index("dp"), lax.axis_index("seq")
    at, core = place // 2, place % 2
    lines = out.shape[1]
    here = pl.ds(pl.multiple_of(pl.program_id(0) * lines, lines), lines)
    copies = []
    for ref, (dp_step, core_step, steps) in zip(pieces, slots):
        for i, k in enumerate(steps):
            owner = ((at_dp ^ dp_step) * 4 + (at ^ k)) * 2 + (core ^ core_step)
            copies.append(
                pltpu.make_async_copy(ref.at[i, here], out.at[owner], sems.at[len(copies)])
            )
    for copy in copies:
        copy.start()
    for copy in copies:
        copy.wait()


def place(pieces, time):
    arrays = [piece[0] for piece in pieces]
    rows = arrays[0].shape[1]
    steps = 4
    return pl.pallas_call(
        functools.partial(place_kernel, slots=tuple(piece[1:] for piece in pieces)),
        grid=(steps,),
        in_specs=[pl.BlockSpec(memory_space=pl.ANY)] * len(arrays),
        out_specs=pl.BlockSpec((GROUPS, rows // steps, CB), lambda i: (0, i, 0)),
        out_shape=jax.ShapeDtypeStruct((GROUPS, rows, CB), BF16),
        scratch_shapes=[pltpu.SemaphoreType.DMA((GROUPS,))],
        compiler_params=params(),
        cost_estimate=cost(time),
        name="place",
    )(*arrays)


def spread_line(bundle):
    count = lax.axis_size("seq") // 2
    return jnp.stack([bundle] + [permute(bundle, 0, 2 * k) for k in range(1, count)], axis=0)


def spread_near(line):
    return permute(line, 1, 0), permute(line, 2, 0)


def spread_far(near):
    half = near[0].shape[0] // 2
    return permute(near[0][:half], 2, 0), permute(near[1][half:], 1, 0)


def to_core(pieces):
    return tuple(permute(piece, 0, 1) for piece in pieces)


def placed(line, near, far, line_c, near_c, far_c, time):
    every, low, high = (0, 1, 2, 3), (0, 1), (2, 3)
    return place(
        [
            (line, 0, 0, every), (near[0], 1, 0, every), (near[1], 2, 0, every),
            (far[0], 3, 0, low), (far[1], 3, 0, high),
            (line_c, 0, 1, every), (near_c[0], 1, 1, every), (near_c[1], 2, 1, every),
            (far_c[0], 3, 1, low), (far_c[1], 3, 1, high),
        ],
        time,
    )


def gather(value):
    return lax.all_gather(value, AXES, axis=0, tiled=False)


def scatter(value):
    return lax.psum_scatter(value, AXES, scatter_dimension=0, tiled=True).astype(F32)


def regroup(full, sections):
    fold = full.shape[0] // GROUPS
    if fold == 1:
        return full
    parts, at = [], 0
    for blocks, rows in sections:
        part = full[:, at : at + blocks * rows].reshape(GROUPS, fold, blocks, rows, CB)
        parts.append(part.swapaxes(1, 2).reshape(GROUPS, blocks * fold * rows, CB))
        at += blocks * rows
    return jnp.concatenate(parts, axis=1)


def joined(mine, other):
    return jnp.stack([mine, other], axis=1).reshape((GROUPS,) + mine.shape[1:])


def permute(value, dp_step, seq_step):
    n_dp, n_seq = lax.axis_size("dp"), lax.axis_size("seq")
    route = [
        (a * n_seq + b, (a ^ dp_step) * n_seq + (b ^ seq_step))
        for a in range(n_dp)
        for b in range(n_seq)
    ]
    return lax.ppermute(value, AXES, route)


def total(parts):
    return functools.reduce(lambda a, b: a + b, [part.astype(F32) for part in parts])


def after(values, *others):
    return lax.optimization_barrier((values, others))[0]


def pick(value, index, axis=0):
    return lax.dynamic_index_in_dim(value, index, axis, keepdims=False)


def meet_core(halves):
    mine, came = halves
    n_dp, at = lax.axis_size("dp"), lax.axis_index("dp")
    shape = (n_dp, mine.shape[0] // n_dp) + mine.shape[1:]
    mine, came = mine.reshape(shape), came.reshape(shape)
    return [total([pick(mine, at ^ m), pick(came, at ^ m)]).astype(BF16) for m in range(n_dp)]


def send_far(parts):
    half = parts[3].shape[0] // 2
    return permute(parts[3][:half], 1, 0), permute(parts[3][half:], 2, 0)


def meet_far(parts, far):
    half = parts[3].shape[0] // 2
    one = jnp.concatenate(
        [parts[1][:half], total([parts[1][half:], far[1]]).astype(BF16)], axis=0
    )
    two = jnp.concatenate(
        [total([parts[2][:half], far[0]]).astype(BF16), parts[2][half:]], axis=0
    )
    return one, two


def send_near(pair):
    return permute(pair[0], 1, 0), permute(pair[1], 2, 0)


def meet_near(own, near):
    at, count = lax.axis_index("seq") // 2, own.shape[0]
    parts = (own,) + tuple(near)
    return [total([pick(part, at ^ k) for part in parts]).astype(BF16) for k in range(count)]


def send_line(parts):
    return [permute(parts[k], 0, 2 * k) for k in range(1, len(parts))]


def meet_line(parts, came):
    return total([parts[0]] + list(came))


def column_blocks(shard, width):
    rows, columns = shard.shape
    return jnp.concatenate([shard[:, c : c + width] for c in range(0, columns, width)], axis=0)


def from_column_blocks(blocks, rows):
    return jnp.concatenate(
        [blocks[r : r + rows] for r in range(0, blocks.shape[0], rows)], axis=1
    )


def mask_table(flags, tail):
    rows = flags.shape[0]
    extended = jnp.concatenate([tail, flags])
    columns = [flags]
    valid = jnp.ones_like(flags)
    for k in range(1, CONV):
        valid = valid * (1.0 - extended[CONV - k : CONV - k + rows])
        columns.append(valid)
    table = jnp.stack(columns, axis=1)
    run = rows // SUB
    tiles = table.reshape(SUB, run, CONV)
    ahead = jnp.concatenate(
        [tiles[1:, : CONV - 1], jnp.zeros((1, CONV - 1, CONV), F32)], axis=0
    )
    tiles = jnp.concatenate([tiles, ahead], axis=1)
    table = tiles.swapaxes(0, 1).reshape((run + CONV - 1) * SUB, CONV)
    return jnp.pad(table, ((0, 0), (0, SUB - CONV)))


def back_edge(ret):
    count = lax.axis_size("seq")
    return lax.ppermute(ret, "seq", [(i + 1, i) for i in range(count - 1)])


def undo_down(value, width):
    rows = value.shape[-2] * FB // width
    rest = value[..., rows:, :]
    rest = jnp.concatenate([rest[..., p * CB : (p + 1) * CB] for p in range(3)], axis=-2)
    return jnp.concatenate([value[..., :rows, :], rest], axis=-1)


def undo_out(value, width):
    own = value.shape[-2]
    rest = value[..., width:]
    rest = jnp.concatenate([rest[..., : own // 2, :], rest[..., own // 2 :, :]], axis=-1)
    return jnp.concatenate([value[..., :width], rest], axis=-2)


def vector_sums(sums, gain2_part, mine):
    devices = lax.axis_size("dp") * lax.axis_size("seq")
    sums = sums.reshape(SUB, devices, mine).swapaxes(0, 1).reshape(devices, SUB * mine)
    return jnp.concatenate([sums, gain2_part[0].reshape(devices, -1)], axis=1)


def plain_back(
    grads_m, do1, full1, full2, yp, h, abar, tot, n1, n1_halo, z,
    xc, ent, xb, gate_pair, small, mask, x, dx1, gain1, gain2_part, mine,
):
    width, lru = n1.shape[1], abar.shape[1]
    dh, dyp, back = turn(do1, full2, yp, h, abar, tot)
    behind = exchange(back[SUB : SUB + 2])
    both, dn1 = side(n1, dyp, full2, z, do1, GROUPS)
    dxb, dpair, sums, ret = rear(
        dh, xc, abar, h, ent, xb, gate_pair, small, mask, back, tot, behind, 0, lru // CB
    )
    last_mine, last_other = weigh(n1, n1_halo, dxb, ret, dpair)
    tokens_grad = last(dxb, back_edge(ret), full1, dn1, x, dx1, gain1)
    gu_mine, gu_other, down_mine, down_other = grads_m
    own = width // GROUPS
    gu = joined(gu_mine, gu_other).reshape(GROUPS, -1, 2, own, FB)
    gate, up = (gu[:, :, i].swapaxes(1, 2).reshape(width, -1) for i in range(2))
    bundle = joined(last_mine, last_other)
    vectors = vector_sums(sums, gain2_part, mine)
    grads = (
        scatter(gate), scatter(up),
        scatter(undo_down(joined(down_mine, down_other), width).reshape(-1, width)),
        scatter(both[:, :own].reshape(width, lru)),
        scatter(undo_out(both[:, own:], width).reshape(lru, width)),
        scatter(bundle[:, :own].reshape(width, lru)),
        scatter(dpair.astype(BF16)),
    )
    return grads, scatter(vectors).reshape(-1), tokens_grad


def staged_back(
    grads_m, do1, full1, full2, yp, h, abar, tot, n1, n1_halo, z,
    xc, ent, xb, gate_pair, small, mask, x, dx1, gain1, gain2_part, mine,
):
    devices, per = GROUPS, n1.shape[1] // GROUPS
    lru = abar.shape[1]
    blocks = lru // CB
    gu_mine, gu_other, down_mine, down_other = grads_m
    sent_gu, sent_down = permute(gu_other, 0, 1), permute(down_other, 0, 1)
    dh, dyp, back = turn(do1, full2, yp, h, abar, tot)
    sent_gu, sent_down, back = after((sent_gu, sent_down, back))
    behind = exchange(back[SUB : SUB + 2])
    parts_m = [
        jnp.concatenate(pair, axis=1)
        for pair in zip(meet_core((gu_mine, sent_gu)), meet_core((down_mine, sent_down)))
    ]
    parts_m, dyp = after((parts_m, dyp))
    far_m = send_far(parts_m)
    both, dn1 = side(n1, dyp, full2, z, do1, devices)
    far_m, behind, dn1 = after((far_m, behind, dn1))
    sum_b = lax.psum_scatter(both, AXES, scatter_dimension=0, tiled=False)
    pair_m = meet_far(parts_m, far_m)
    pair_m, dh = after((pair_m, dh))
    near_m = send_near(pair_m)
    dxb, dpair, sums, ret = rear(
        dh, xc, abar, h, ent, xb, gate_pair, small, mask, back, tot, behind, 0, blocks
    )
    last_mine, last_other = weigh(n1, n1_halo, dxb, ret, dpair)
    near_m, last_mine, last_other, ret = after((near_m, last_mine, last_other, ret))
    line_m = meet_near(parts_m[0], near_m)
    sent_m = send_line(line_m)
    ret = back_edge(ret)
    flat = vector_sums(sums, gain2_part, mine)
    lines = mine // blocks
    flat = jnp.pad(flat, ((0, 0), (0, lines * lru - flat.shape[1])))
    flat = flat.astype(BF16).reshape(devices // 2, 2, lines, lru)
    core = lax.axis_index("seq") % 2
    last_mine = lax.dynamic_update_slice(last_mine, pick(flat, core, 1), (0, per + lines, 0))
    last_other = lax.dynamic_update_slice(last_other, pick(flat, 1 - core, 1), (0, per + lines, 0))
    sent_l = permute(last_other, 0, 1)
    parts_l = meet_core((last_mine, sent_l))
    far_l = send_far(parts_l)
    parts_l, line_m, dxb = after((parts_l, line_m, dxb))
    tokens_grad = last(dxb, ret, full1, dn1, x, dx1, gain1)
    far_l, tokens_grad = after((far_l, tokens_grad))
    pair_l = meet_far(parts_l, far_l)
    near_l = send_near(pair_l)
    near_l, sent_m = after((near_l, sent_m))
    sum_m = meet_line(line_m, sent_m)
    count_m = gu_mine.shape[1]
    gu = sum_m[:count_m].reshape(-1, 2, per, FB)
    mlp_gate_grad = gu[:, 0].swapaxes(0, 1).reshape(per, -1)
    mlp_up_grad = gu[:, 1].swapaxes(0, 1).reshape(per, -1)
    mlp_down_grad = undo_down(sum_m[count_m:], n1.shape[1])
    line_l = meet_near(parts_l[0], near_l)
    sent_line_l, sum_b = after((send_line(line_l), sum_b))
    sum_b = sum_b.astype(F32)
    gelu_branch_grad, mixer_out_grad = sum_b[:per], undo_out(sum_b[per:], n1.shape[1])
    bundle = meet_line(line_l, sent_line_l)
    recur_in_grad = bundle[:per]
    pair = bundle[per : per + lines].reshape(lines, blocks, CB).swapaxes(0, 1).reshape(mine, CB)
    flat = bundle[per + lines :].reshape(-1)
    grads = (
        mlp_gate_grad, mlp_up_grad, mlp_down_grad, gelu_branch_grad, mixer_out_grad, recur_in_grad, pair,
    )
    return grads, flat, tokens_grad


def on_device(
    tokens, seg_starts, cotangent, recur_in, gelu_branch, mixer_out, conv_weight, conv_bias,
    rate_gate, input_gate, rate_bias, input_bias, decay_param, mixer_gain, mlp_gate, mlp_up,
    mlp_down, mlp_gain,
):
    rows, width = tokens.shape
    devices = lax.axis_size("dp") * lax.axis_size("seq")
    count = lax.axis_size("seq")
    lru = recur_in.shape[1]
    mine = conv_bias.shape[0]
    share = mixer_gain.shape[0]

    per = recur_in.shape[0]
    blocks = lru // CB
    across = lambda array, rows: jnp.pad(array, ((0, rows - array.shape[0]), (0, CB - array.shape[1])))
    vectors = jnp.concatenate(
        [
            across(
                jnp.concatenate(
                    [conv_weight, conv_bias[None], rate_bias[None], input_bias[None], decay_param[None]],
                    axis=0,
                ),
                SUB,
            ),
            across(jnp.stack([mixer_gain, mlp_gain], axis=0), SUB),
        ],
        axis=0,
    )
    hidden = mlp_gate.shape[1]
    flags = seg_starts.astype(F32)
    pair = jnp.concatenate([rate_gate, input_gate], axis=1)
    lag = CONV - 1
    tail = jnp.concatenate(
        [tokens[rows - lag :], jnp.pad(flags[rows - lag :].astype(BF16), (0, width - lag))[None]], axis=0
    )
    send_on = lambda value: lax.ppermute(value, "seq", [(i, i + 1) for i in range(count - 1)])
    if staged():
        (first,) = pack([recur_in, pair, vectors])
        line1 = spread_line(first)
        second, third = pack([gelu_branch, mixer_out], [mlp_gate, mlp_up, mlp_down])
        tail = send_on(after(tail, first))
        line1, second, tail = after((line1, second, tail))
        near1 = spread_near(line1)
        line2 = spread_line(second)
        far1 = spread_far(near1)
        line1, near1_b, line2 = after((line1, near1, line2))
        full3 = gather(after(third, near1_b))
        line1_c, near1_c = to_core((line1,))[0], to_core(near1_b)
        far1, line1_c, near1_c, line2 = after((far1, line1_c, near1_c, line2))
        far1_c = to_core(far1)
        far1_c, line2 = after((far1_c, line2))
        near2 = spread_near(line2)
        full1 = placed(line1, near1, far1, line1_c, near1_c, far1_c, 4)
    else:
        full1 = gather(jnp.concatenate([column_blocks(recur_in, CB), pair, vectors], axis=0))
        tail = send_on(tail)
    x_halo, flag_tail = tail[:lag], tail[lag, :lag].astype(F32)
    mask = mask_table(flags, flag_tail)
    pair_at = per * blocks
    raw = full1
    gate_pair = raw[:, pair_at : pair_at + mine].reshape(lru, 2 * HEAD)
    small = raw[:, pair_at + mine : pair_at + mine + SUB, :mine].astype(F32)
    small = small.swapaxes(0, 1).reshape(SUB, lru)
    gain1, gain2 = (
        raw[:, pair_at + mine + SUB + i, :share].astype(F32).reshape(1, width) for i in range(2)
    )
    small = jnp.concatenate([small[:7], -RATE_SCALE * jax.nn.softplus(-small[7:8])], axis=0)
    full1 = regroup(raw, [(blocks, per)])

    x = interleave(tokens)
    g = interleave(cotangent)
    x_halo = jnp.pad(x_halo[::-1], ((0, 16 - (CONV - 1)), (0, 0)))

    n1, xb, xc, abar, drive, tot, n1_halo = front(x, x_halo, gain1, full1, gate_pair, small, mask)
    ahead = tot[2 * SUB : 2 * SUB + 2]
    if staged():
        near2, ahead = after((near2, ahead))
        far2 = spread_far(near2)
        line2_c, near2_c = to_core((line2,))[0], to_core(near2)
        ahead = exchange(ahead)
        far2, line2_c, near2_c, ahead = after((far2, line2_c, near2_c, ahead))
        far2_c = to_core(far2)
        full2 = placed(line2, near2, far2, line2_c, near2_c, far2_c, 5)
    else:
        ahead = exchange(ahead)
        second = jnp.concatenate([column_blocks(gelu_branch, CB), column_blocks(mixer_out, CB)], axis=0)
        full2 = regroup(gather(second), [(blocks, per), (width // CB, mine)])
    yp = branch(n1, full2, lru)
    h, z, x1, n2, ent = mix(abar, drive, yp, x, full2, tot, ahead, gain2)
    if not staged():
        third = [column_blocks(array, CB) for array in (mlp_gate, mlp_up, mlp_down)]
        full3 = regroup(
            gather(jnp.concatenate(third)),
            [(hidden // CB, per), (hidden // CB, per), (width // CB, hidden // devices)],
        )
    out, dx1, do1, gain2_part, *grads_m = mlp(
        n2, g, full3, hidden, 0, hidden // FB, None, [x1, gain2]
    )
    grads, flat, tokens_grad = (staged_back if staged() else plain_back)(
        grads_m, do1, full1, full2, yp, h, abar, tot, n1, n1_halo, z,
        xc, ent, xb, gate_pair, small, mask, x, dx1, gain1, gain2_part, mine,
    )
    mlp_gate_grad, mlp_up_grad, mlp_down_grad, gelu_branch_grad, mixer_out_grad, recur_in_grad, pair = grads
    by_gain = sum(
        jnp.sum(weight.astype(F32) * grad, axis=1)
        for weight, grad in ((recur_in, recur_in_grad), (gelu_branch, gelu_branch_grad))
    )
    gain1_grad = by_gain / mixer_gain.astype(F32)
    row = lambda r: flat[r * mine : (r + 1) * mine]
    decay_grad = RATE_SCALE * jax.nn.sigmoid(-decay_param.astype(F32)) * row(2)
    gain_at = SUB * mine
    return (
        uninterleave(out),
        uninterleave(tokens_grad),
        recur_in_grad,
        gelu_branch_grad,
        mixer_out_grad,
        flat[4 * mine : 8 * mine].reshape(CONV, mine),
        row(3),
        pair[:, :HEAD],
        pair[:, HEAD:],
        row(0),
        row(1),
        decay_grad,
        gain1_grad,
        mlp_gate_grad,
        mlp_up_grad,
        mlp_down_grad,
        flat[gain_at : gain_at + share],
    )


def solution(mesh):
    both, alone = P(AXES, None), P(AXES)
    across = P(None, AXES)
    return jax.shard_map(
        on_device,
        mesh=mesh,
        in_specs=(
            both, alone, both, both, both, both, across, alone, both, both, alone, alone, alone,
            alone, both, both, both, alone,
        ),
        out_specs=(
            both, both, both, both, both, across, alone, both, both, alone, alone, alone, alone,
            both, both, both, alone,
        ),
        check_vma=False,
    )
```

```python
import functools

import jax
import jax.numpy as jnp
from jax import lax
from jax.experimental import pallas as pl
from jax.experimental.pallas import tpu as pltpu
from jax.sharding import PartitionSpec as P

AXES = ("dp", "seq")
CONV = 4
EPSILON = 1e-06
RATE_SCALE = 8.0
SUB = 8
CB = 256
HEAD = 128
LEAD = 32
STEP = 128
WIDE = 512
TALL = 512
FB = 768
VMEM = 60 * 1024 * 1024
GROUPS = 32
GELU_C = 0.7978845608028654
GELU_K = 0.044715
F32 = jnp.float32
BF16 = jnp.bfloat16


def params(**extra):
    return pltpu.CompilerParams(vmem_limit_bytes=VMEM, **extra)


def cost(time):
    return pl.CostEstimate(flops=int(time * 1e6), bytes_accessed=0, transcendentals=0)


def once(shape, index_map):
    return pl.BlockSpec(shape, index_map, pipeline_mode=pl.Buffered(1))


def dot(left, right):
    return jnp.dot(left, right, preferred_element_type=F32)


def dot_t(left, right):
    return lax.dot_general(left, right, (((1,), (1,)), ((), ())), preferred_element_type=F32)


def t_dot(left, right):
    return lax.dot_general(left, right, (((0,), (0,)), ((), ())), preferred_element_type=F32)


def staged():
    return lax.axis_size("dp") == 4 and lax.axis_size("dp") * lax.axis_size("seq") == GROUPS


def parity():
    return lax.axis_index("seq") % 2 if staged() else 0


def halves(core, value, pairs):
    value = value.astype(BF16).reshape(pairs, 2, value.shape[0] // (2 * pairs), value.shape[-1])
    zero, one = value[:, 0], value[:, 1]
    return jnp.where(core == 0, zero, one), jnp.where(core == 0, one, zero)


def split(core, value, mine_ref, other_ref, rows):
    mine_ref[:, rows, :], other_ref[:, rows, :] = halves(core, value, mine_ref.shape[0])


def gelu_parts(v):
    square = v * v
    tanh = jnp.tanh(v * (GELU_C + (GELU_C * GELU_K) * square))
    half = 0.5 + 0.5 * tanh
    slope = half + (0.5 * v) * (1.0 - tanh * tanh) * (GELU_C + (3.0 * GELU_C * GELU_K) * square)
    return v * half, slope


def gelu_value(v):
    tanh = jnp.tanh(v * (GELU_C + (GELU_C * GELU_K) * (v * v)))
    return v * (0.5 + 0.5 * tanh)


def decay_parts(rate, neg_soft, flag):
    log_decay = rate * neg_soft
    decay = jnp.exp(log_decay)
    y = 2.0 * log_decay
    series = 1.0 / 720.0
    for k in (120.0, 24.0, 6.0, 2.0, 1.0):
        series = 1.0 / k + y * series
    gap = jnp.where(y > -0.3, -y * series, 1.0 - decay * decay)
    inverse = lax.rsqrt(jnp.maximum(gap, 1e-30))
    return decay, inverse, jnp.where(flag > 0.5, 1.0, gap * inverse)


def sigmoid(v):
    return 0.5 + 0.5 * jnp.tanh(0.5 * v)


def gates(conv_low, gate_ref, small_ref):
    one = dot(conv_low[:, :HEAD], gate_ref[:HEAD, :])
    two = dot(conv_low[:, HEAD:], gate_ref[HEAD:, :])
    rate = sigmoid(
        jnp.concatenate([one[:, :HEAD], two[:, :HEAD]], axis=1) + small_ref[5:6, :]
    )
    enter = sigmoid(
        jnp.concatenate([one[:, HEAD:], two[:, HEAD:]], axis=1) + small_ref[6:7, :]
    )
    return rate, enter


def front_kernel(
    x_ref, xh_ref, gain_ref, w_ref, g_ref, small_ref, mask_ref,
    n1_ref, xb_ref, xc_ref, ab_ref, drive_ref, tot_ref, n1h_ref,
    e_ref,
):
    rows = x_ref.shape[0]

    @pl.when(pl.program_id(0) == 0)
    def _():
        gain = gain_ref[0:1, :]

        def norm(i, carry):
            at = pl.ds(pl.multiple_of(i * STEP, STEP), STEP)
            x = x_ref[at, :].astype(F32)
            scale = lax.rsqrt(jnp.mean(x * x, axis=-1, keepdims=True) + EPSILON)
            n1_ref[at, :] = (x * scale * gain).astype(BF16)
            return carry

        lax.fori_loop(0, rows // STEP, norm, 0)
        xh = xh_ref[...].astype(F32)
        scale = lax.rsqrt(jnp.mean(xh * xh, axis=-1, keepdims=True) + EPSILON)
        n1h_ref[...] = (xh * scale * gain).astype(BF16)

    weight = w_ref[...].reshape(n1_ref.shape[1], CB)

    half = rows // 4
    for i in range(4):
        part = dot(n1_ref[i * half : (i + 1) * half, :], weight).astype(BF16).astype(F32)
        e_ref[LEAD + i * half : LEAD + (i + 1) * half, :] = part
    halo = dot(n1h_ref[...], weight).astype(BF16).astype(F32)
    first = lax.broadcasted_iota(jnp.int32, (SUB, CB), 0) == 0
    e_ref[0:SUB, :] = jnp.zeros((SUB, CB), F32)
    for q in range(1, CONV):
        tile = e_ref[LEAD + rows - SUB * q : LEAD + rows - SUB * (q - 1), :]
        tile = pltpu.roll(tile, 1, 0)
        e_ref[LEAD - SUB * q : LEAD - SUB * (q - 1), :] = jnp.where(
            first, jnp.broadcast_to(halo[q - 1 : q, :], (SUB, CB)), tile
        )
    xb_ref[...] = e_ref[...].astype(BF16)

    def chunk(i, carry):
        base = pl.multiple_of(i * WIDE, WIDE)
        at = pl.ds(base, WIDE)
        mask = mask_ref[at, :]
        total = small_ref[4:5, :] + small_ref[0:1, :] * e_ref[pl.ds(base + LEAD, WIDE), :]
        for k in range(1, CONV):
            shifted = e_ref[pl.ds(base + LEAD - SUB * k, WIDE), :]
            total = total + (small_ref[k : k + 1, :] * mask[:, k : k + 1]) * shifted
        low = total.astype(BF16)
        xc_ref[at, :] = low
        rate, enter = gates(low, g_ref, small_ref)
        flag = mask[:, 0:1]
        decay, _, multiplier = decay_parts(rate, small_ref[7:8, :], flag)
        drive = multiplier * enter * low.astype(F32)
        abar = decay * (1.0 - flag)
        ab_ref[at, :] = abar
        drive_ref[at, :] = drive
        product, state = carry
        for t in range(WIDE // SUB):
            a = abar[t * SUB : (t + 1) * SUB, :]
            product = product * a
            state = state * a + drive[t * SUB : (t + 1) * SUB, :]
        return product, state

    start = (jnp.ones((SUB, CB), F32), jnp.zeros((SUB, CB), F32))
    product, state = lax.fori_loop(0, rows // WIDE, chunk, start)
    tot_ref[0:SUB, :] = product
    tot_ref[SUB : 2 * SUB, :] = state
    whole_p, whole_s = product[0:1, :], state[0:1, :]
    for s in range(1, SUB):
        whole_s = whole_s * product[s : s + 1, :] + state[s : s + 1, :]
        whole_p = whole_p * product[s : s + 1, :]
    tot_ref[2 * SUB : 2 * SUB + 1, :] = whole_p
    tot_ref[2 * SUB + 1 : 2 * SUB + 2, :] = whole_s
    tot_ref[2 * SUB + 2 : 3 * SUB, :] = jnp.zeros((SUB - 2, CB), F32)


def front(x, x_halo, gain, recur_blocks, gate_pair, small, mask):
    rows, width = x.shape
    lru = gate_pair.shape[0]
    devices, per = recur_blocks.shape[0], width // recur_blocks.shape[0]
    col = lambda r: pl.BlockSpec((r, CB), lambda j: (0, j))
    return pl.pallas_call(
        front_kernel,
        grid=(lru // CB,),
        in_specs=[
            once((rows, width), lambda j: (0, 0)),
            once(x_halo.shape, lambda j: (0, 0)),
            once((1, width), lambda j: (0, 0)),
            pl.BlockSpec((devices, per, CB), lambda j: (0, j, 0)),
            pl.BlockSpec((CB, 2 * HEAD), lambda j: (j, 0)),
            col(SUB),
            once(mask.shape, lambda j: (0, 0)),
        ],
        out_specs=[
            once((rows, width), lambda j: (0, 0)),
            col(rows + LEAD), col(rows), col(rows), col(rows), col(3 * SUB),
            once(x_halo.shape, lambda j: (0, 0)),
        ],
        out_shape=[
            jax.ShapeDtypeStruct((rows, width), BF16),
            jax.ShapeDtypeStruct((rows + LEAD, lru), BF16),
            jax.ShapeDtypeStruct((rows, lru), BF16),
            jax.ShapeDtypeStruct((rows, lru), F32),
            jax.ShapeDtypeStruct((rows, lru), F32),
            jax.ShapeDtypeStruct((3 * SUB, lru), F32),
            jax.ShapeDtypeStruct(x_halo.shape, BF16),
        ],
        scratch_shapes=[pltpu.VMEM((rows + LEAD, CB), F32)],
        compiler_params=params(),
        cost_estimate=cost(33),
        name="front",
    )(x, x_halo, gain, recur_blocks, gate_pair, small, mask)


def branch_kernel(n_ref, w_ref, out_ref):
    out_ref[...] = dot(n_ref[...], w_ref[...].reshape(n_ref.shape[1], CB)).astype(BF16)


def branch(n1, bundle, lru):
    rows, width = n1.shape
    devices, steps = bundle.shape[0], lru // CB
    own = width // devices
    return pl.pallas_call(
        branch_kernel,
        grid=(lru // CB,),
        in_specs=[
            once((rows, width), lambda j: (0, 0)),
            pl.BlockSpec((devices, own, CB), lambda j: (0, j, 0)),
        ],
        out_specs=pl.BlockSpec((rows, CB), lambda j: (0, j)),
        out_shape=jax.ShapeDtypeStruct((rows, lru), BF16),
        compiler_params=params(),
        cost_estimate=cost(8),
        name="branch",
    )(n1, bundle)


def mix_kernel(*refs, pieces):
    ab_ref, drive_ref, yp_ref, x_ref, w0_ref, w1_ref, w2_ref, w3_ref, tot_ref, gain_ref = refs[:10]
    piece_refs = refs[10 : 10 + pieces]
    h_ref, z_ref, x1_ref, n2_ref, ent_ref, state_ref, piece_ref = refs[-7:]
    rows = ab_ref.shape[0]

    @pl.when(pl.program_id(0) == 0)
    def _():
        for k, ref in enumerate(piece_refs):
            piece_ref[k * SUB : (k + 1) * SUB, :] = ref[...]
        enter = fold_before(piece_ref)
        for s in range(SUB):
            ent_ref[s : s + 1, :] = enter
            enter = tot_ref[s : s + 1, :] * enter + tot_ref[SUB + s : SUB + s + 1, :]
        state_ref[...] = ent_ref[...]

    def tiles(i, state):
        at = pl.ds(pl.multiple_of(i * 2 * SUB, 2 * SUB), 2 * SUB)
        a, d = ab_ref[at, :], drive_ref[at, :]
        one = a[:SUB, :] * state + d[:SUB, :]
        two = a[SUB:, :] * one + d[SUB:, :]
        h = jnp.concatenate([one, two], axis=0)
        h_ref[at, :] = h.astype(BF16)
        z_ref[at, :] = (h * gelu_value(yp_ref[at, :].astype(F32))).astype(BF16)
        return two

    state_ref[...] = lax.fori_loop(0, rows // (2 * SUB), tiles, state_ref[...])
    z = z_ref[...]
    mixed = [dot(z, w[...].reshape(z.shape[1], CB)) for w in (w0_ref, w1_ref, w2_ref, w3_ref)]
    x1 = x_ref[...].astype(F32) + jnp.concatenate(mixed, axis=1)
    x1_ref[...] = x1
    scale = lax.rsqrt(jnp.mean(x1 * x1, axis=-1, keepdims=True) + EPSILON)
    n2_ref[...] = (x1 * scale * gain_ref[0:1, :]).astype(BF16)


def out_blocks(bundle, lru, width):
    devices = bundle.shape[0]
    own, ahead = lru // devices, (lru // CB) * (width // devices) // (lru // devices)
    return [
        once((devices, own, CB), lambda i, c=c: (0, ahead + c, 0)) for c in range(width // CB)
    ]


def mix(abar, drive, yp, x, bundle, tot, pieces, gain):
    rows, lru = abar.shape
    width = x.shape[1]
    weights = out_blocks(bundle, lru, width)
    block = 256
    row = lambda w: pl.BlockSpec((block, w), lambda i: (i, 0))
    whole = lambda a: once(a.shape, lambda i: (0, 0))
    return pl.pallas_call(
        functools.partial(mix_kernel, pieces=len(pieces)),
        grid=(rows // block,),
        in_specs=[
            row(lru), row(lru), row(lru), row(width),
            *weights, whole(tot), whole(gain), *[whole(piece) for piece in pieces],
        ],
        out_specs=[row(lru), row(lru), row(width), row(width), pl.BlockSpec((SUB, lru), lambda i: (0, 0))],
        out_shape=[
            jax.ShapeDtypeStruct((rows, lru), BF16),
            jax.ShapeDtypeStruct((rows, lru), BF16),
            jax.ShapeDtypeStruct((rows, width), F32),
            jax.ShapeDtypeStruct((rows, width), BF16),
            jax.ShapeDtypeStruct((SUB, lru), F32),
        ],
        scratch_shapes=[
            pltpu.VMEM((SUB, lru), F32), pltpu.VMEM((SUB * len(pieces), lru), F32),
        ],
        compiler_params=params(),
        cost_estimate=cost(15),
        name="mix",
    )(abar, drive, yp, x, *[bundle] * len(weights), tot, gain, *pieces)


def mlp_kernel(*refs, begins, ends):
    n_ref, g_ref, gate_ref, up_ref, d0_ref, d1_ref, d2_ref, d3_ref = refs[:8]
    refs = refs[8:]
    if not begins:
        acc_in_ref, dx_in_ref, _, _ = refs[:4]
        refs = refs[4:]
    if ends:
        x1_hbm, gain_ref, out_ref, dx_ref, do_ref, gg_ref = refs[:6]
        refs = refs[6:]
    else:
        acc_ref, dx_ref = refs[:2]
        refs = refs[2:]
    gu_mine_ref, gu_other_ref, down_mine_ref, down_other_ref = refs[:4]
    nt_ref, mm_ref, dl_ref, wt_ref, dt_ref = refs[4:9]
    if ends:
        acc_ref, x1_ref, x1_sem = refs[9:12]
    rows, width = n_ref.shape
    step = TALL
    j = pl.program_id(0)

    @pl.when(j == 0)
    def _():
        nt_ref[...] = n_ref[...].T
        if begins:
            acc_ref[...] = jnp.zeros_like(acc_ref)
            dx_ref[...] = jnp.zeros_like(dx_ref)
        else:
            acc_ref[...] = acc_in_ref[...]
            dx_ref[...] = dx_in_ref[...]

    own = gate_ref.shape[1] * CB // FB
    for p in range(FB // CB):
        here = slice(p * own, (p + 1) * own)
        wt_ref[:, p * CB : (p + 1) * CB] = gate_ref[:, here, :].reshape(width, CB)
        wt_ref[:, FB + p * CB : FB + (p + 1) * CB] = up_ref[:, here, :].reshape(width, CB)
    for c, ref in enumerate((d0_ref, d1_ref, d2_ref, d3_ref)):
        dt_ref[:, c * CB : (c + 1) * CB] = ref[...].reshape(FB, CB)

    def part(i, carry):
        at = pl.ds(pl.multiple_of(i * step, step), step)
        n, g = n_ref[at, :], g_ref[at, :]
        both = dot(n, wt_ref[...])
        gate_act, slope = gelu_parts(both[:, :FB])
        up = both[:, FB:]
        mm = (gate_act * up).astype(BF16)
        mm_ref[at, :] = mm
        grad = dot_t(g, dt_ref[...])
        dl_ref[at, :FB] = (grad * up * slope).astype(BF16)
        dl_ref[at, FB:] = (grad * gate_act).astype(BF16)
        acc_ref[at, :] += dot(mm, dt_ref[...])
        dx_ref[at, :] += dot_t(dl_ref[at, :], wt_ref[...])
        return carry

    lax.fori_loop(0, rows // step, part, 0, unroll=True)
    core = parity()
    per = gu_mine_ref.shape[1] // 2
    split(core, dot(nt_ref[...], dl_ref[:, :FB]), gu_mine_ref, gu_other_ref, slice(0, per))
    split(core, dot(nt_ref[...], dl_ref[:, FB:]), gu_mine_ref, gu_other_ref, slice(per, 2 * per))
    downs = halves(core, t_dot(mm_ref[...], g_ref[...]), down_mine_ref.shape[0])
    for owned, ref in zip(downs, (down_mine_ref, down_other_ref)):
        rows_own = owned.shape[1]
        ref[:, :rows_own, :] = owned[:, :, :FB]
        third = rows_own // 3
        for p in range(3):
            ref[:, rows_own:, p * CB : (p + 1) * CB] = owned[:, p * third : (p + 1) * third, FB:]

    if ends:

        @pl.when(j == pl.num_programs(0) - 1)
        def _():
            gain = gain_ref[0:1, :]

            def fetch(i):
                at = pl.ds(pl.multiple_of(i * STEP, STEP), STEP)
                slot = lax.rem(i, 2)
                return pltpu.make_async_copy(x1_hbm.at[at], x1_ref.at[slot], x1_sem.at[slot])

            fetch(0).start()

            def close(i, total):
                at = pl.ds(pl.multiple_of(i * STEP, STEP), STEP)

                @pl.when(i + 1 < rows // STEP)
                def _():
                    fetch(i + 1).start()

                fetch(i).wait()
                x1 = x1_ref[lax.rem(i, 2)]
                out_ref[at, :] = (x1 + acc_ref[at, :]).astype(BF16)
                scale = lax.rsqrt(jnp.mean(x1 * x1, axis=-1, keepdims=True) + EPSILON)
                q = x1 * scale
                dn = dx_ref[at, :]
                w = dn * gain
                inner = jnp.mean(w * q, axis=-1, keepdims=True)
                dx = g_ref[at, :].astype(F32) + scale * (w - q * inner)
                dx_ref[at, :] = dx
                do_ref[at, :] = dx.astype(BF16)
                return total + jnp.sum(dn * q, axis=0, keepdims=True)

            gg_ref[...] = jnp.broadcast_to(
                lax.fori_loop(0, rows // STEP, close, jnp.zeros((1, width), F32)), gg_ref.shape
            )


def mlp(n2, g, bundle, hidden, start, count, before=None, close=None):
    rows, width = n2.shape
    devices, steps = bundle.shape[0], hidden // FB
    own, per = width // devices, hidden // devices
    group = FB // per
    whole = lambda s: once(s, lambda j: (0, 0))
    lines = own * (FB // CB)
    gate = pl.BlockSpec((devices, lines, CB), lambda j: (0, start + j, 0))
    up = pl.BlockSpec((devices, lines, CB), lambda j: (0, steps + start + j, 0))
    downs = [
        pl.BlockSpec((group, per, CB), lambda j, c=c: (start + j, 2 * steps * lines // per + c, 0))
        for c in range(width // CB)
    ]
    pair = pl.BlockSpec((devices // 2, 2 * own, FB), lambda j: (0, j, 0))
    lines_down = per * width // FB
    half = pl.BlockSpec((group // 2, lines_down, FB), lambda j: (start + j, 0, 0))
    operands = [n2, g, bundle, bundle, *[bundle] * len(downs)]
    in_specs = [whole(n2.shape), whole(g.shape), gate, up, *downs]
    shape_f = jax.ShapeDtypeStruct((rows, width), F32)
    shape_b = jax.ShapeDtypeStruct((rows, width), BF16)
    aliases = {}
    if before is not None:
        operands += before
        in_specs += [whole(shape_f.shape)] * 2 + [pl.BlockSpec(memory_space=pl.ANY)] * 2
    if close is not None:
        operands += close
        in_specs += [pl.BlockSpec(memory_space=pl.ANY), whole(close[1].shape)]
        outs = [shape_b, shape_f, shape_b, jax.ShapeDtypeStruct((SUB, width), F32)]
    else:
        outs = [shape_f, shape_f]
    out_specs = [whole(shape.shape) for shape in outs]
    if before is not None:
        aliases = {10: len(outs) + 2, 11: len(outs) + 3}
    gu = jax.ShapeDtypeStruct((devices // 2, 2 * own * count, FB), BF16)
    down = jax.ShapeDtypeStruct((devices // 2, lines_down, FB), BF16)
    return pl.pallas_call(
        functools.partial(mlp_kernel, begins=before is None, ends=close is not None),
        grid=(count,),
        in_specs=in_specs,
        out_specs=out_specs + [pair, pair, half, half],
        out_shape=outs + [gu, gu, down, down],
        scratch_shapes=[
            pltpu.VMEM((width, rows), BF16),
            pltpu.VMEM((rows, FB), BF16),
            pltpu.VMEM((rows, 2 * FB), BF16),
            pltpu.VMEM((width, 2 * FB), BF16),
            pltpu.VMEM((FB, width), BF16),
        ]
        + (
            [
                pltpu.VMEM((rows, width), F32),
                pltpu.VMEM((2, STEP, width), F32),
                pltpu.SemaphoreType.DMA((2,)),
            ]
            if close is not None
            else []
        ),
        input_output_aliases=aliases,
        compiler_params=params(),
        cost_estimate=cost(20 * count),
        name="mlp",
    )(*operands)


def turn_kernel(
    do_ref, w0_ref, w1_ref, w2_ref, w3_ref, yp_ref, h_ref, ab_ref, tot_ref,
    dh_ref, dyp_ref, back_ref,
    dz_ref, w_ref,
):
    rows, width = do_ref.shape

    @pl.when(pl.program_id(0) == 0)
    def _():
        for c, ref in enumerate((w0_ref, w1_ref, w2_ref, w3_ref)):
            w_ref[:, c * CB : (c + 1) * CB] = ref[...].reshape(w_ref.shape[0], CB)

    weight = w_ref[pl.ds(pl.multiple_of(pl.program_id(0) * CB, CB), CB), :]
    half = rows // 4
    for i in range(4):
        dz_ref[i * half : (i + 1) * half, :] = dot_t(do_ref[i * half : (i + 1) * half, :], weight)

    def chunk(i, carry):
        base = pl.multiple_of((rows // WIDE - 1 - i) * WIDE, WIDE)
        at = pl.ds(base, WIDE)
        dz = dz_ref[at, :]
        act, slope = gelu_parts(yp_ref[at, :].astype(F32))
        dh = dz * act
        dh_ref[at, :] = dh
        dyp_ref[at, :] = (dz * h_ref[at, :].astype(F32) * slope).astype(BF16)
        abar = ab_ref[at, :]
        leave = carry
        for t in reversed(range(WIDE // SUB)):
            here = slice(t * SUB, (t + 1) * SUB)
            leave = abar[here, :] * (dh[here, :] + leave)
        return leave

    leave = lax.fori_loop(0, rows // WIDE, chunk, jnp.zeros((SUB, CB), F32))
    back_ref[0:SUB, :] = leave
    whole = leave[SUB - 1 : SUB, :]
    for s in reversed(range(SUB - 1)):
        whole = whole * tot_ref[s : s + 1, :] + leave[s : s + 1, :]
    back_ref[SUB : SUB + 1, :] = tot_ref[2 * SUB : 2 * SUB + 1, :]
    back_ref[SUB + 1 : SUB + 2, :] = whole
    back_ref[SUB + 2 : 2 * SUB, :] = jnp.zeros((SUB - 2, CB), F32)


def turn(do1, bundle, yp, h, abar, tot):
    rows, width = do1.shape
    lru = abar.shape[1]
    weights = out_blocks(bundle, lru, width)
    col = lambda r: pl.BlockSpec((r, CB), lambda j: (0, j))
    return pl.pallas_call(
        turn_kernel,
        grid=(lru // CB,),
        in_specs=[
            once((rows, width), lambda j: (0, 0)),
            *weights,
            col(rows), col(rows), col(rows), col(3 * SUB),
        ],
        out_specs=[col(rows), col(rows), col(2 * SUB)],
        out_shape=[
            jax.ShapeDtypeStruct((rows, lru), F32),
            jax.ShapeDtypeStruct((rows, lru), BF16),
            jax.ShapeDtypeStruct((2 * SUB, lru), F32),
        ],
        scratch_shapes=[pltpu.VMEM((rows, CB), F32), pltpu.VMEM((lru, width), BF16)],
        compiler_params=params(),
        cost_estimate=cost(15),
        name="turn",
    )(do1, *[bundle] * len(weights), yp, h, abar, tot)


def side_kernel(
    n_ref, dyp_ref, w_ref, z_ref, do_ref,
    both_ref, dn_ref,
    nt_ref,
):
    @pl.when(pl.program_id(0) == 0)
    def _():
        nt_ref[...] = n_ref[...].T
        dn_ref[...] = jnp.zeros_like(dn_ref)

    j = pl.program_id(0)
    width, block = n_ref.shape[1], dyp_ref.shape[1]
    own = w_ref.shape[1] * CB // block
    columns = pl.ds(pl.multiple_of(j * block, block), block)
    devices = both_ref.shape[0]
    both_ref[:, :own, columns] = dot(nt_ref[...], dyp_ref[...]).astype(BF16).reshape(devices, own, block)
    for p in range(block // CB):
        weight = w_ref[:, p * own : (p + 1) * own, :].reshape(width, CB)
        dn_ref[...] += dot_t(dyp_ref[:, p * CB : (p + 1) * CB], weight)
    half = devices // 2
    there = pl.ds(pl.multiple_of(j * half, half), half)
    out = t_dot(z_ref[...], do_ref[...]).astype(BF16).reshape(half, block // half, width)
    both_ref[there, own : 2 * own, :width] = out[:, :own, :]
    both_ref[there, own : own + own // 2, width:] = out[:, own:, : width // 2]
    both_ref[there, own + own // 2 : 2 * own, width:] = out[:, own:, width // 2 :]


def side(n1, dyp, weight, z, do1, devices):
    rows, width = n1.shape
    lru = dyp.shape[1]
    block = lru // 2
    both = (devices, 2 * (width // devices), lru)
    whole = once((rows, width), lambda j: (0, 0))
    col = pl.BlockSpec((rows, block), lambda j: (0, j))
    return pl.pallas_call(
        side_kernel,
        grid=(lru // block,),
        in_specs=[
            whole, col,
            pl.BlockSpec((devices, block // CB * (width // devices), CB), lambda j: (0, j, 0)),
            col, whole,
        ],
        out_specs=[once(both, lambda j: (0, 0, 0)), whole],
        out_shape=[
            jax.ShapeDtypeStruct(both, BF16),
            jax.ShapeDtypeStruct((rows, width), F32),
        ],
        scratch_shapes=[pltpu.VMEM((width, rows), BF16)],
        compiler_params=params(),
        cost_estimate=cost(16),
        name="side",
    )(n1, dyp, weight, z, do1)


def rear_kernel(*refs, pieces):
    dh_ref, xc_ref, ab_ref, h_ref, ent_ref, xb_ref, g_ref, small_ref, mask_ref, back_ref, tot_ref = refs[:11]
    piece_refs = refs[11 : 11 + pieces]
    dxb_ref, dg_ref, sum_ref, ret_ref, cin_ref, dxc_ref, dl_ref, piece_ref = refs[-8:]
    rows = dh_ref.shape[0]
    for k, ref in enumerate(piece_refs):
        piece_ref[k * SUB : (k + 1) * SUB, :] = ref[...]
    neg_soft = small_ref[7:8, :]

    leave = fold_after(piece_ref)
    for s in reversed(range(SUB)):
        cin_ref[s : s + 1, :] = leave
        leave = tot_ref[s : s + 1, :] * leave + back_ref[s : s + 1, :]

    def chunk(i, carry):
        leave, sums = carry
        base = pl.multiple_of((rows // rows - 1 - i) * rows, rows)
        at = pl.ds(base, rows)
        mask = mask_ref[at, :]
        flag = mask[:, 0:1]
        low = xc_ref[at, :]
        conv = low.astype(F32)
        rate, enter = gates(low, g_ref, small_ref)
        decay, inverse, multiplier = decay_parts(rate, neg_soft, flag)
        abar = ab_ref[at, :]
        dh = dh_ref[at, :]
        parts = []
        for t in reversed(range(rows // SUB)):
            here = slice(t * SUB, (t + 1) * SUB)
            delta = dh[here, :] + leave
            leave = abar[here, :] * delta
            parts.append(delta)
        delta = jnp.concatenate(parts[::-1], axis=0)
        now = h_ref[at, :].astype(F32)
        before_at = pl.ds(pl.multiple_of(jnp.maximum(base - 2 * SUB, 0), 2 * SUB), 2 * SUB)
        before = h_ref[before_at, :].astype(F32)[SUB:, :]
        before = jnp.where(base == 0, ent_ref[...], before)
        prior = jnp.concatenate([before, now[: rows - SUB, :]], axis=0)
        gated = delta * enter
        dla = (1.0 - flag) * decay * (delta * prior - gated * conv * (decay * inverse))
        by_rate = dla * rate
        dr = neg_soft * by_rate * (1.0 - rate)
        scaled = delta * multiplier
        di = scaled * conv * enter * (1.0 - enter)
        drl, dil = dr.astype(BF16), di.astype(BF16)
        one = jnp.concatenate([drl[:, :HEAD], dil[:, :HEAD]], axis=1)
        two = jnp.concatenate([drl[:, HEAD:], dil[:, HEAD:]], axis=1)
        dl_ref[at, : 2 * HEAD] = one
        dl_ref[at, 2 * HEAD :] = two
        through = jnp.concatenate(
            [dot_t(one, g_ref[:HEAD, :]), dot_t(two, g_ref[HEAD:, :])], axis=1
        )
        dxc = scaled * enter + through
        dxc_ref[at, :] = dxc
        fold = lambda v: functools.reduce(
            lambda a, b: a + b, [v[t * SUB : (t + 1) * SUB, :] for t in range(rows // SUB)]
        )
        new = [fold(dr), fold(di), fold(by_rate), fold(dxc)]
        for k in range(CONV):
            more = 2 * SUB * (k % 2)
            lines = pl.ds(pl.multiple_of(base + LEAD - SUB * (k + k % 2), 2 * SUB), rows + more)
            shift = xb_ref[lines, :].astype(F32)[more // 2 : more // 2 + rows, :]
            term = dxc * shift
            if k:
                term = term * mask[:, k : k + 1]
            new.append(fold(term))
        return leave, tuple(a + b for a, b in zip(sums, new))

    zero = jnp.zeros((SUB, CB), F32)
    _, sums = lax.fori_loop(0, rows // rows, chunk, (cin_ref[...], (zero,) * 8))
    for r, value in enumerate(sums):
        sum_ref[r : r + 1, :] = jnp.sum(value, axis=0, keepdims=True)

    for q in range(CONV - 1):
        tile = dxc_ref[q * SUB : (q + 1) * SUB, :]
        dxc_ref[rows + q * SUB : rows + (q + 1) * SUB, :] = pltpu.roll(tile, SUB - 1, 0)
    for q in range(1, CONV):
        back = jnp.zeros((1, CB), F32)
        for k in range(q, CONV):
            t = (k - q) * SUB
            back = back + small_ref[k : k + 1, :] * mask_ref[t : t + 1, k : k + 1] * dxc_ref[t : t + 1, :]
        ret_ref[q - 1 : q, :] = back
    ret_ref[CONV - 1 :, :] = jnp.zeros((SUB - CONV + 1, CB), F32)

    def spread(i, carry):
        base = pl.multiple_of(i * rows, rows)
        total = small_ref[0:1, :] * dxc_ref[pl.ds(base, rows), :]
        for k in range(1, CONV):
            at = pl.ds(base + SUB * k, rows)
            total = total + (small_ref[k : k + 1, :] * mask_ref[at, k : k + 1]) * dxc_ref[at, :]
        dxb_ref[pl.ds(base, rows), :] = total.astype(BF16)
        return carry

    lax.fori_loop(0, rows // rows, spread, 0)
    dg_ref[:HEAD, :] = t_dot(xc_ref[:, :HEAD], dl_ref[:, : 2 * HEAD])
    dg_ref[HEAD:, :] = t_dot(xc_ref[:, HEAD:], dl_ref[:, 2 * HEAD :])


def rear(dh, xc, abar, h, ent, xb, gate_pair, small, mask, back, tot, pieces, start, count, before=()):
    rows, lru = dh.shape
    col = lambda r: pl.BlockSpec((r, CB), lambda j: (0, start + j))
    pair = pl.BlockSpec((CB, 2 * HEAD), lambda j: (start + j, 0))
    operands = [dh, xc, abar, h, ent, xb, gate_pair, small, mask, back, tot, *pieces, *before]
    return pl.pallas_call(
        functools.partial(rear_kernel, pieces=len(pieces)),
        grid=(count,),
        in_specs=[
            col(rows), col(rows), col(rows), col(rows), col(SUB), col(rows + LEAD), pair, col(SUB),
            once(mask.shape, lambda j: (0, 0)),
            col(2 * SUB), col(3 * SUB),
        ]
        + [col(SUB)] * len(pieces)
        + [pl.BlockSpec(memory_space=pl.ANY)] * len(before),
        out_specs=[col(rows), pair, col(SUB), col(SUB)],
        out_shape=[
            jax.ShapeDtypeStruct((rows, lru), BF16),
            jax.ShapeDtypeStruct((lru, 2 * HEAD), F32),
            jax.ShapeDtypeStruct((SUB, lru), F32),
            jax.ShapeDtypeStruct((SUB, lru), F32),
        ],
        scratch_shapes=[
            pltpu.VMEM((SUB, CB), F32),
            pltpu.VMEM((rows + LEAD, CB), F32),
            pltpu.VMEM((rows, 4 * HEAD), BF16),
            pltpu.VMEM((SUB * len(pieces), CB), F32),
        ],
        input_output_aliases={len(operands) - len(before) + i: i for i in range(len(before))},
        compiler_params=params(),
        cost_estimate=cost(7 * count),
        name="rear",
    )(*operands)


def with_edge(dxb_ref, ret_ref):
    rows, width = dxb_ref.shape
    lastly = lax.broadcasted_iota(jnp.int32, (SUB, width), 0) == SUB - 1
    tail = dxb_ref[rows - 4 * SUB :, :].astype(F32)
    tiles = [tail[:SUB, :]]
    for q in reversed(range(1, CONV)):
        tile = tail[(4 - q) * SUB : (5 - q) * SUB, :]
        tiles.append(tile + jnp.where(lastly, ret_ref[q - 1 : q, :], 0.0))
    return jnp.concatenate(tiles, axis=0).astype(BF16)


def weigh_kernel(n_ref, nh_ref, d_ref, ret_ref, dp_ref, mine_ref, other_ref, nt_ref):
    @pl.when(pl.program_id(0) == 0)
    def _():
        nt_ref[...] = n_ref[...].T

    width = n_ref.shape[1]
    core = parity()
    per = width // (2 * mine_ref.shape[0])
    edge = jnp.concatenate([ret_ref[...], jnp.zeros_like(ret_ref)], axis=0).astype(BF16)
    grad = dot(nt_ref[...], d_ref[...]) + t_dot(nh_ref[...], edge)
    split(core, grad, mine_ref, other_ref, slice(0, per))
    devices, lines, wide = dp_ref.shape
    pair = jnp.concatenate([dp_ref[...], jnp.zeros_like(dp_ref)], axis=1)
    split(core, pair.reshape(devices * 2 * lines, wide), mine_ref, other_ref, slice(per, per + 2 * lines))


def weigh(n1, n1_halo, dxb, ret, dpair):
    rows, width = n1.shape
    lru = dxb.shape[1]
    devices, per = GROUPS, width // GROUPS
    col = lambda r: pl.BlockSpec((r, CB), lambda j: (0, j))
    lines = lru // devices // (lru // CB)
    dpair = dpair.reshape(devices, lru // devices, 2 * HEAD)
    bundle = pl.BlockSpec((devices // 2, per + 2 * lines, CB), lambda j: (0, 0, j))
    shape = jax.ShapeDtypeStruct((devices // 2, per + 2 * lines, lru), BF16)
    return pl.pallas_call(
        weigh_kernel,
        grid=(lru // CB,),
        in_specs=[
            once(n1.shape, lambda j: (0, 0)), once(n1_halo.shape, lambda j: (0, 0)), col(rows), col(SUB),
            pl.BlockSpec((devices, lines, 2 * HEAD), lambda j: (0, j, 0)),
        ],
        out_specs=[bundle, bundle],
        out_shape=[shape, shape],
        scratch_shapes=[pltpu.VMEM((width, rows), BF16)],
        compiler_params=params(),
        cost_estimate=cost(8),
        name="weigh",
    )(n1, n1_halo, dxb, ret, dpair)


def last_kernel(d_ref, ret_ref, w_ref, dn_ref, x_ref, dx_ref, gain_ref, out_ref, wt_ref, e_ref):
    rows, width = x_ref.shape
    block = 256

    @pl.when(pl.program_id(0) == 0)
    def _():
        own = w_ref.shape[1] * CB // wt_ref.shape[1]
        for p in range(wt_ref.shape[1] // CB):
            here = slice(p * own, (p + 1) * own)
            wt_ref[:, p * CB : (p + 1) * CB] = w_ref[:, here, :].reshape(width, CB)

    x = x_ref[...].astype(F32)
    scale = lax.rsqrt(jnp.mean(x * x, axis=-1, keepdims=True) + EPSILON)
    q = x * scale
    e_ref[...] = d_ref[...]

    @pl.when(pl.program_id(0) == pl.num_programs(0) - 1)
    def _():
        e_ref[rows - 4 * SUB :, :] = with_edge(d_ref, ret_ref)

    dn = dn_ref[...] + dot_t(e_ref[...], wt_ref[...])
    w = dn * gain_ref[0:1, :]
    inner = jnp.mean(w * q, axis=-1, keepdims=True)
    out_ref[...] = (dx_ref[...] + scale * (w - q * inner)).astype(BF16)


def last(dxb, ret, recur_blocks, dn, x, dx1, gain):
    rows, lru = dxb.shape
    width = x.shape[1]
    devices, per = recur_blocks.shape[0], width // recur_blocks.shape[0]
    block = 256
    row = lambda w: pl.BlockSpec((block, w), lambda i: (i, 0))
    return pl.pallas_call(
        last_kernel,
        grid=(rows // block,),
        in_specs=[
            row(lru), once(ret.shape, lambda i: (0, 0)),
            once((devices, per * (lru // CB), CB), lambda i: (0, 0, 0)),
            row(width), row(width), row(width), once(gain.shape, lambda i: (0, 0)),
        ],
        out_specs=row(width),
        out_shape=jax.ShapeDtypeStruct(x.shape, BF16),
        scratch_shapes=[pltpu.VMEM((width, lru), BF16), pltpu.VMEM((block, lru), BF16)],
        compiler_params=params(),
        cost_estimate=cost(11),
        name="last",
    )(dxb, ret, recur_blocks, dn, x, dx1, gain)


def interleave(values):
    return values.reshape((SUB, values.shape[0] // SUB) + values.shape[1:]).swapaxes(0, 1).reshape(values.shape)


def uninterleave(values):
    return values.reshape((values.shape[0] // SUB, SUB) + values.shape[1:]).swapaxes(0, 1).reshape(values.shape)


def exchange(value):
    core = lax.axis_index("seq") % 2
    came = permute(value, 0, 1)
    pair = jnp.concatenate(
        [
            jnp.where(core == 0, value, came),
            jnp.where(core == 0, came, value),
            jnp.zeros((SUB - 2 * value.shape[0],) + value.shape[1:], value.dtype),
        ],
        axis=0,
    )
    count = lax.axis_size("seq") // 2
    return [pair] + [permute(pair, 0, 2 * k) for k in range(1, count)]


def fold_before(piece_ref):
    place = lax.axis_index("seq")
    at = place // 2
    value = jnp.zeros((1, piece_ref.shape[1]), F32)
    for k in range(piece_ref.shape[0] // SUB):
        rows = piece_ref[pl.ds(pl.multiple_of((at ^ k) * SUB, SUB), SUB), :]
        value = jnp.where(2 * k < place, rows[0:1, :] * value + rows[1:2, :], value)
        value = jnp.where(2 * k + 1 < place, rows[2:3, :] * value + rows[3:4, :], value)
    return value


def fold_after(piece_ref):
    place = lax.axis_index("seq")
    at = place // 2
    value = jnp.zeros((1, piece_ref.shape[1]), F32)
    for k in reversed(range(piece_ref.shape[0] // SUB)):
        rows = piece_ref[pl.ds(pl.multiple_of((at ^ k) * SUB, SUB), SUB), :]
        value = jnp.where(2 * k + 1 > place, rows[2:3, :] * value + rows[3:4, :], value)
        value = jnp.where(2 * k > place, rows[0:1, :] * value + rows[1:2, :], value)
    return value


def pack_kernel(*refs, layout):
    outs = refs[len(refs) - len({at[0] for at in layout}) :]
    for out, row, source, column in layout:
        block = refs[source][:, column : column + CB]
        outs[out][row : row + block.shape[0], :] = block


def pack(*bundles):
    layout, sources, shapes = [], [], []
    for out, arrays in enumerate(bundles):
        row = 0
        for array in arrays:
            for column in range(0, array.shape[1], CB):
                layout.append((out, row, len(sources), column))
                row += array.shape[0]
            sources.append(array)
        shapes.append(jax.ShapeDtypeStruct((row, CB), BF16))
    return pl.pallas_call(
        functools.partial(pack_kernel, layout=tuple(layout)),
        out_shape=shapes,
        compiler_params=params(),
        cost_estimate=cost(2),
        name="pack",
    )(*sources)


def place_kernel(*refs, slots):
    pieces, out, sems = refs[: len(slots)], refs[len(slots)], refs[len(slots) + 1]
    at_dp, place = lax.axis_index("dp"), lax.axis_index("seq")
    at, core = place // 2, place % 2
    lines = out.shape[1]
    here = pl.ds(pl.multiple_of(pl.program_id(0) * lines, lines), lines)
    copies = []
    for ref, (dp_step, core_step, steps) in zip(pieces, slots):
        for i, k in enumerate(steps):
            owner = ((at_dp ^ dp_step) * 4 + (at ^ k)) * 2 + (core ^ core_step)
            copies.append(
                pltpu.make_async_copy(ref.at[i, here], out.at[owner], sems.at[len(copies)])
            )
    for copy in copies:
        copy.start()
    for copy in copies:
        copy.wait()


def place(pieces, time):
    arrays = [piece[0] for piece in pieces]
    rows = arrays[0].shape[1]
    steps = 4
    return pl.pallas_call(
        functools.partial(place_kernel, slots=tuple(piece[1:] for piece in pieces)),
        grid=(steps,),
        in_specs=[pl.BlockSpec(memory_space=pl.ANY)] * len(arrays),
        out_specs=pl.BlockSpec((GROUPS, rows // steps, CB), lambda i: (0, i, 0)),
        out_shape=jax.ShapeDtypeStruct((GROUPS, rows, CB), BF16),
        scratch_shapes=[pltpu.SemaphoreType.DMA((GROUPS,))],
        compiler_params=params(),
        cost_estimate=cost(time),
        name="place",
    )(*arrays)


def spread_line(bundle):
    count = lax.axis_size("seq") // 2
    return jnp.stack([bundle] + [permute(bundle, 0, 2 * k) for k in range(1, count)], axis=0)


def spread_near(line):
    return permute(line, 1, 0), permute(line, 2, 0)


def spread_far(near):
    half = near[0].shape[0] // 2
    return permute(near[0][:half], 2, 0), permute(near[1][half:], 1, 0)


def to_core(pieces):
    return tuple(permute(piece, 0, 1) for piece in pieces)


def placed(line, near, far, line_c, near_c, far_c, time):
    every, low, high = (0, 1, 2, 3), (0, 1), (2, 3)
    return place(
        [
            (line, 0, 0, every), (near[0], 1, 0, every), (near[1], 2, 0, every),
            (far[0], 3, 0, low), (far[1], 3, 0, high),
            (line_c, 0, 1, every), (near_c[0], 1, 1, every), (near_c[1], 2, 1, every),
            (far_c[0], 3, 1, low), (far_c[1], 3, 1, high),
        ],
        time,
    )


def gather(value):
    return lax.all_gather(value, AXES, axis=0, tiled=False)


def scatter(value):
    return lax.psum_scatter(value, AXES, scatter_dimension=0, tiled=True).astype(F32)


def regroup(full, sections):
    fold = full.shape[0] // GROUPS
    if fold == 1:
        return full
    parts, at = [], 0
    for blocks, rows in sections:
        part = full[:, at : at + blocks * rows].reshape(GROUPS, fold, blocks, rows, CB)
        parts.append(part.swapaxes(1, 2).reshape(GROUPS, blocks * fold * rows, CB))
        at += blocks * rows
    return jnp.concatenate(parts, axis=1)


def joined(mine, other):
    return jnp.stack([mine, other], axis=1).reshape((GROUPS,) + mine.shape[1:])


def permute(value, dp_step, seq_step):
    n_dp, n_seq = lax.axis_size("dp"), lax.axis_size("seq")
    route = [
        (a * n_seq + b, (a ^ dp_step) * n_seq + (b ^ seq_step))
        for a in range(n_dp)
        for b in range(n_seq)
    ]
    return lax.ppermute(value, AXES, route)


def total(parts):
    return functools.reduce(lambda a, b: a + b, [part.astype(F32) for part in parts])


def after(values, *others):
    return lax.optimization_barrier((values, others))[0]


def pick(value, index, axis=0):
    return lax.dynamic_index_in_dim(value, index, axis, keepdims=False)


def meet_core(halves):
    mine, came = halves
    n_dp, at = lax.axis_size("dp"), lax.axis_index("dp")
    shape = (n_dp, mine.shape[0] // n_dp) + mine.shape[1:]
    mine, came = mine.reshape(shape), came.reshape(shape)
    return [total([pick(mine, at ^ m), pick(came, at ^ m)]).astype(BF16) for m in range(n_dp)]


def send_far(parts):
    half = parts[3].shape[0] // 2
    return permute(parts[3][:half], 1, 0), permute(parts[3][half:], 2, 0)


def meet_far(parts, far):
    half = parts[3].shape[0] // 2
    one = jnp.concatenate(
        [parts[1][:half], total([parts[1][half:], far[1]]).astype(BF16)], axis=0
    )
    two = jnp.concatenate(
        [total([parts[2][:half], far[0]]).astype(BF16), parts[2][half:]], axis=0
    )
    return one, two


def send_near(pair):
    return permute(pair[0], 1, 0), permute(pair[1], 2, 0)


def meet_near(own, near):
    at, count = lax.axis_index("seq") // 2, own.shape[0]
    parts = (own,) + tuple(near)
    return [total([pick(part, at ^ k) for part in parts]).astype(BF16) for k in range(count)]


def send_line(parts):
    return [permute(parts[k], 0, 2 * k) for k in range(1, len(parts))]


def meet_line(parts, came):
    return total([parts[0]] + list(came))


def column_blocks(shard, width):
    rows, columns = shard.shape
    return jnp.concatenate([shard[:, c : c + width] for c in range(0, columns, width)], axis=0)


def from_column_blocks(blocks, rows):
    return jnp.concatenate(
        [blocks[r : r + rows] for r in range(0, blocks.shape[0], rows)], axis=1
    )


def mask_table(flags, tail):
    rows = flags.shape[0]
    extended = jnp.concatenate([tail, flags])
    columns = [flags]
    valid = jnp.ones_like(flags)
    for k in range(1, CONV):
        valid = valid * (1.0 - extended[CONV - k : CONV - k + rows])
        columns.append(valid)
    table = jnp.stack(columns, axis=1)
    run = rows // SUB
    tiles = table.reshape(SUB, run, CONV)
    ahead = jnp.concatenate(
        [tiles[1:, : CONV - 1], jnp.zeros((1, CONV - 1, CONV), F32)], axis=0
    )
    tiles = jnp.concatenate([tiles, ahead], axis=1)
    table = tiles.swapaxes(0, 1).reshape((run + CONV - 1) * SUB, CONV)
    return jnp.pad(table, ((0, 0), (0, SUB - CONV)))


def back_edge(ret):
    count = lax.axis_size("seq")
    return lax.ppermute(ret, "seq", [(i + 1, i) for i in range(count - 1)])


def undo_down(value, width):
    rows = value.shape[-2] * FB // width
    rest = value[..., rows:, :]
    rest = jnp.concatenate([rest[..., p * CB : (p + 1) * CB] for p in range(3)], axis=-2)
    return jnp.concatenate([value[..., :rows, :], rest], axis=-1)


def undo_out(value, width):
    own = value.shape[-2]
    rest = value[..., width:]
    rest = jnp.concatenate([rest[..., : own // 2, :], rest[..., own // 2 :, :]], axis=-1)
    return jnp.concatenate([value[..., :width], rest], axis=-2)


def vector_sums(sums, gain2_part, mine):
    devices = lax.axis_size("dp") * lax.axis_size("seq")
    sums = sums.reshape(SUB, devices, mine).swapaxes(0, 1).reshape(devices, SUB * mine)
    return jnp.concatenate([sums, gain2_part[0].reshape(devices, -1)], axis=1)


def plain_back(
    grads_m, do1, full1, full2, yp, h, abar, tot, n1, n1_halo, z,
    xc, ent, xb, gate_pair, small, mask, x, dx1, gain1, gain2_part, mine,
):
    width, lru = n1.shape[1], abar.shape[1]
    dh, dyp, back = turn(do1, full2, yp, h, abar, tot)
    behind = exchange(back[SUB : SUB + 2])
    both, dn1 = side(n1, dyp, full2, z, do1, GROUPS)
    dxb, dpair, sums, ret = rear(
        dh, xc, abar, h, ent, xb, gate_pair, small, mask, back, tot, behind, 0, lru // CB
    )
    last_mine, last_other = weigh(n1, n1_halo, dxb, ret, dpair)
    tokens_grad = last(dxb, back_edge(ret), full1, dn1, x, dx1, gain1)
    gu_mine, gu_other, down_mine, down_other = grads_m
    own = width // GROUPS
    gu = joined(gu_mine, gu_other).reshape(GROUPS, -1, 2, own, FB)
    gate, up = (gu[:, :, i].swapaxes(1, 2).reshape(width, -1) for i in range(2))
    bundle = joined(last_mine, last_other)
    vectors = vector_sums(sums, gain2_part, mine)
    grads = (
        scatter(gate), scatter(up),
        scatter(undo_down(joined(down_mine, down_other), width).reshape(-1, width)),
        scatter(both[:, :own].reshape(width, lru)),
        scatter(undo_out(both[:, own:], width).reshape(lru, width)),
        scatter(bundle[:, :own].reshape(width, lru)),
        scatter(dpair.astype(BF16)),
    )
    return grads, scatter(vectors).reshape(-1), tokens_grad


def staged_back(
    grads_m, do1, full1, full2, yp, h, abar, tot, n1, n1_halo, z,
    xc, ent, xb, gate_pair, small, mask, x, dx1, gain1, gain2_part, mine,
):
    devices, per = GROUPS, n1.shape[1] // GROUPS
    lru = abar.shape[1]
    blocks = lru // CB
    gu_mine, gu_other, down_mine, down_other = grads_m
    sent_gu, sent_down = permute(gu_other, 0, 1), permute(down_other, 0, 1)
    dh, dyp, back = turn(do1, full2, yp, h, abar, tot)
    sent_gu, sent_down, back = after((sent_gu, sent_down, back))
    behind = exchange(back[SUB : SUB + 2])
    parts_m = [
        jnp.concatenate(pair, axis=1)
        for pair in zip(meet_core((gu_mine, sent_gu)), meet_core((down_mine, sent_down)))
    ]
    parts_m, dyp = after((parts_m, dyp))
    far_m = send_far(parts_m)
    both, dn1 = side(n1, dyp, full2, z, do1, devices)
    far_m, behind, dn1 = after((far_m, behind, dn1))
    sum_b = lax.psum_scatter(both, AXES, scatter_dimension=0, tiled=False)
    pair_m = meet_far(parts_m, far_m)
    pair_m, dh = after((pair_m, dh))
    near_m = send_near(pair_m)
    dxb, dpair, sums, ret = rear(
        dh, xc, abar, h, ent, xb, gate_pair, small, mask, back, tot, behind, 0, blocks
    )
    last_mine, last_other = weigh(n1, n1_halo, dxb, ret, dpair)
    near_m, last_mine, last_other, ret = after((near_m, last_mine, last_other, ret))
    line_m = meet_near(parts_m[0], near_m)
    sent_m = send_line(line_m)
    ret = back_edge(ret)
    flat = vector_sums(sums, gain2_part, mine)
    lines = mine // blocks
    flat = jnp.pad(flat, ((0, 0), (0, lines * lru - flat.shape[1])))
    flat = flat.astype(BF16).reshape(devices // 2, 2, lines, lru)
    core = lax.axis_index("seq") % 2
    last_mine = lax.dynamic_update_slice(last_mine, pick(flat, core, 1), (0, per + lines, 0))
    last_other = lax.dynamic_update_slice(last_other, pick(flat, 1 - core, 1), (0, per + lines, 0))
    sent_l = permute(last_other, 0, 1)
    parts_l = meet_core((last_mine, sent_l))
    far_l = send_far(parts_l)
    parts_l, line_m, dxb = after((parts_l, line_m, dxb))
    tokens_grad = last(dxb, ret, full1, dn1, x, dx1, gain1)
    far_l, tokens_grad = after((far_l, tokens_grad))
    pair_l = meet_far(parts_l, far_l)
    near_l = send_near(pair_l)
    near_l, sent_m = after((near_l, sent_m))
    sum_m = meet_line(line_m, sent_m)
    count_m = gu_mine.shape[1]
    gu = sum_m[:count_m].reshape(-1, 2, per, FB)
    mlp_gate_grad = gu[:, 0].swapaxes(0, 1).reshape(per, -1)
    mlp_up_grad = gu[:, 1].swapaxes(0, 1).reshape(per, -1)
    mlp_down_grad = undo_down(sum_m[count_m:], n1.shape[1])
    line_l = meet_near(parts_l[0], near_l)
    sent_line_l = send_line(line_l)
    sum_b = sum_b.astype(F32)
    gelu_branch_grad, mixer_out_grad = sum_b[:per], undo_out(sum_b[per:], n1.shape[1])
    sent_line_l = after(sent_line_l, (gelu_branch_grad, mixer_out_grad))
    bundle = meet_line(line_l, sent_line_l)
    recur_in_grad = bundle[:per]
    pair = bundle[per : per + lines].reshape(lines, blocks, CB).swapaxes(0, 1).reshape(mine, CB)
    flat = bundle[per + lines :].reshape(-1)
    grads = (
        mlp_gate_grad, mlp_up_grad, mlp_down_grad, gelu_branch_grad, mixer_out_grad, recur_in_grad, pair,
    )
    return grads, flat, tokens_grad


def on_device(
    tokens, seg_starts, cotangent, recur_in, gelu_branch, mixer_out, conv_weight, conv_bias,
    rate_gate, input_gate, rate_bias, input_bias, decay_param, mixer_gain, mlp_gate, mlp_up,
    mlp_down, mlp_gain,
):
    rows, width = tokens.shape
    devices = lax.axis_size("dp") * lax.axis_size("seq")
    count = lax.axis_size("seq")
    lru = recur_in.shape[1]
    mine = conv_bias.shape[0]
    share = mixer_gain.shape[0]

    per = recur_in.shape[0]
    blocks = lru // CB
    across = lambda array, rows: jnp.pad(array, ((0, rows - array.shape[0]), (0, CB - array.shape[1])))
    vectors = jnp.concatenate(
        [
            across(
                jnp.concatenate(
                    [conv_weight, conv_bias[None], rate_bias[None], input_bias[None], decay_param[None]],
                    axis=0,
                ),
                SUB,
            ),
            across(jnp.stack([mixer_gain, mlp_gain], axis=0), SUB),
        ],
        axis=0,
    )
    hidden = mlp_gate.shape[1]
    flags = seg_starts.astype(F32)
    pair = jnp.concatenate([rate_gate, input_gate], axis=1)
    lag = CONV - 1
    tail = jnp.concatenate(
        [tokens[rows - lag :], jnp.pad(flags[rows - lag :].astype(BF16), (0, width - lag))[None]], axis=0
    )
    send_on = lambda value: lax.ppermute(value, "seq", [(i, i + 1) for i in range(count - 1)])
    if staged():
        (first,) = pack([recur_in, pair, vectors])
        line1 = spread_line(first)
        second, third = pack([gelu_branch, mixer_out], [mlp_gate, mlp_up, mlp_down])
        tail = send_on(after(tail, first))
        line1, second, tail = after((line1, second, tail))
        near1 = spread_near(line1)
        line2 = spread_line(second)
        far1 = spread_far(near1)
        line1, near1_b, line2 = after((line1, near1, line2))
        full3 = gather(after(third, near1_b))
        line1_c, near1_c = to_core((line1,))[0], to_core(near1_b)
        far1, line1_c, near1_c, line2 = after((far1, line1_c, near1_c, line2))
        far1_c = to_core(far1)
        far1_c, line2 = after((far1_c, line2))
        near2 = spread_near(line2)
        full1 = placed(line1, near1, far1, line1_c, near1_c, far1_c, 4)
    else:
        full1 = gather(jnp.concatenate([column_blocks(recur_in, CB), pair, vectors], axis=0))
        tail = send_on(tail)
    x_halo, flag_tail = tail[:lag], tail[lag, :lag].astype(F32)
    mask = mask_table(flags, flag_tail)
    pair_at = per * blocks
    raw = full1
    gate_pair = raw[:, pair_at : pair_at + mine].reshape(lru, 2 * HEAD)
    small = raw[:, pair_at + mine : pair_at + mine + SUB, :mine].astype(F32)
    small = small.swapaxes(0, 1).reshape(SUB, lru)
    gain1, gain2 = (
        raw[:, pair_at + mine + SUB + i, :share].astype(F32).reshape(1, width) for i in range(2)
    )
    small = jnp.concatenate([small[:7], -RATE_SCALE * jax.nn.softplus(-small[7:8])], axis=0)
    full1 = regroup(raw, [(blocks, per)])

    x = interleave(tokens)
    g = interleave(cotangent)
    x_halo = jnp.pad(x_halo[::-1], ((0, 16 - (CONV - 1)), (0, 0)))

    n1, xb, xc, abar, drive, tot, n1_halo = front(x, x_halo, gain1, full1, gate_pair, small, mask)
    ahead = tot[2 * SUB : 2 * SUB + 2]
    if staged():
        near2, ahead = after((near2, ahead))
        far2 = spread_far(near2)
        line2_c, near2_c = to_core((line2,))[0], to_core(near2)
        ahead = exchange(ahead)
        far2, line2_c, near2_c, ahead = after((far2, line2_c, near2_c, ahead))
        far2_c = to_core(far2)
        full2 = placed(line2, near2, far2, line2_c, near2_c, far2_c, 5)
    else:
        ahead = exchange(ahead)
        second = jnp.concatenate([column_blocks(gelu_branch, CB), column_blocks(mixer_out, CB)], axis=0)
        full2 = regroup(gather(second), [(blocks, per), (width // CB, mine)])
    yp = branch(n1, full2, lru)
    h, z, x1, n2, ent = mix(abar, drive, yp, x, full2, tot, ahead, gain2)
    if not staged():
        third = [column_blocks(array, CB) for array in (mlp_gate, mlp_up, mlp_down)]
        full3 = regroup(
            gather(jnp.concatenate(third)),
            [(hidden // CB, per), (hidden // CB, per), (width // CB, hidden // devices)],
        )
    out, dx1, do1, gain2_part, *grads_m = mlp(
        n2, g, full3, hidden, 0, hidden // FB, None, [x1, gain2]
    )
    grads, flat, tokens_grad = (staged_back if staged() else plain_back)(
        grads_m, do1, full1, full2, yp, h, abar, tot, n1, n1_halo, z,
        xc, ent, xb, gate_pair, small, mask, x, dx1, gain1, gain2_part, mine,
    )
    mlp_gate_grad, mlp_up_grad, mlp_down_grad, gelu_branch_grad, mixer_out_grad, recur_in_grad, pair = grads
    by_gain = sum(
        jnp.sum(weight.astype(F32) * grad, axis=1)
        for weight, grad in ((recur_in, recur_in_grad), (gelu_branch, gelu_branch_grad))
    )
    gain1_grad = by_gain / mixer_gain.astype(F32)
    row = lambda r: flat[r * mine : (r + 1) * mine]
    decay_grad = RATE_SCALE * jax.nn.sigmoid(-decay_param.astype(F32)) * row(2)
    gain_at = SUB * mine
    return (
        uninterleave(out),
        uninterleave(tokens_grad),
        recur_in_grad,
        gelu_branch_grad,
        mixer_out_grad,
        flat[4 * mine : 8 * mine].reshape(CONV, mine),
        row(3),
        pair[:, :HEAD],
        pair[:, HEAD:],
        row(0),
        row(1),
        decay_grad,
        gain1_grad,
        mlp_gate_grad,
        mlp_up_grad,
        mlp_down_grad,
        flat[gain_at : gain_at + share],
    )


def solution(mesh):
    both, alone = P(AXES, None), P(AXES)
    across = P(None, AXES)
    return jax.shard_map(
        on_device,
        mesh=mesh,
        in_specs=(
            both, alone, both, both, both, both, across, alone, both, both, alone, alone, alone,
            alone, both, both, both, alone,
        ),
        out_specs=(
            both, both, both, both, both, across, alone, both, both, alone, alone, alone, alone,
            both, both, both, alone,
        ),
        check_vma=False,
    )
```

```python
import functools

import jax
import jax.numpy as jnp
from jax import lax
from jax.experimental import pallas as pl
from jax.experimental.pallas import tpu as pltpu
from jax.sharding import PartitionSpec as P

AXES = ("dp", "seq")
CONV = 4
EPSILON = 1e-06
RATE_SCALE = 8.0
SUB = 8
CB = 256
HEAD = 128
LEAD = 32
STEP = 128
WIDE = 512
TALL = 512
FB = 768
VMEM = 60 * 1024 * 1024
GROUPS = 32
GELU_C = 0.7978845608028654
GELU_K = 0.044715
F32 = jnp.float32
BF16 = jnp.bfloat16


def params(**extra):
    return pltpu.CompilerParams(vmem_limit_bytes=VMEM, **extra)


def cost(time):
    return pl.CostEstimate(flops=int(time * 1e6), bytes_accessed=0, transcendentals=0)


def once(shape, index_map):
    return pl.BlockSpec(shape, index_map, pipeline_mode=pl.Buffered(1))


def dot(left, right):
    return jnp.dot(left, right, preferred_element_type=F32)


def dot_t(left, right):
    return lax.dot_general(left, right, (((1,), (1,)), ((), ())), preferred_element_type=F32)


def t_dot(left, right):
    return lax.dot_general(left, right, (((0,), (0,)), ((), ())), preferred_element_type=F32)


def staged():
    return lax.axis_size("dp") == 4 and lax.axis_size("dp") * lax.axis_size("seq") == GROUPS


def parity():
    return lax.axis_index("seq") % 2 if staged() else 0


def halves(core, value, pairs):
    value = value.astype(BF16).reshape(pairs, 2, value.shape[0] // (2 * pairs), value.shape[-1])
    zero, one = value[:, 0], value[:, 1]
    return jnp.where(core == 0, zero, one), jnp.where(core == 0, one, zero)


def split(core, value, mine_ref, other_ref, rows):
    mine_ref[:, rows, :], other_ref[:, rows, :] = halves(core, value, mine_ref.shape[0])


def gelu_parts(v):
    square = v * v
    tanh = jnp.tanh(v * (GELU_C + (GELU_C * GELU_K) * square))
    half = 0.5 + 0.5 * tanh
    slope = half + (0.5 * v) * (1.0 - tanh * tanh) * (GELU_C + (3.0 * GELU_C * GELU_K) * square)
    return v * half, slope


def gelu_value(v):
    tanh = jnp.tanh(v * (GELU_C + (GELU_C * GELU_K) * (v * v)))
    return v * (0.5 + 0.5 * tanh)


def decay_parts(rate, neg_soft, flag):
    log_decay = rate * neg_soft
    decay = jnp.exp(log_decay)
    y = 2.0 * log_decay
    series = 1.0 / 720.0
    for k in (120.0, 24.0, 6.0, 2.0, 1.0):
        series = 1.0 / k + y * series
    gap = jnp.where(y > -0.3, -y * series, 1.0 - decay * decay)
    inverse = lax.rsqrt(jnp.maximum(gap, 1e-30))
    return decay, inverse, jnp.where(flag > 0.5, 1.0, gap * inverse)


def sigmoid(v):
    return 0.5 + 0.5 * jnp.tanh(0.5 * v)


def gates(conv_low, gate_ref, small_ref):
    one = dot(conv_low[:, :HEAD], gate_ref[:HEAD, :])
    two = dot(conv_low[:, HEAD:], gate_ref[HEAD:, :])
    rate = sigmoid(
        jnp.concatenate([one[:, :HEAD], two[:, :HEAD]], axis=1) + small_ref[5:6, :]
    )
    enter = sigmoid(
        jnp.concatenate([one[:, HEAD:], two[:, HEAD:]], axis=1) + small_ref[6:7, :]
    )
    return rate, enter


def front_kernel(
    x_ref, xh_ref, gain_ref, w_ref, g_ref, small_ref, mask_ref,
    n1_ref, xb_ref, xc_ref, ab_ref, drive_ref, tot_ref, n1h_ref,
    e_ref,
):
    rows = x_ref.shape[0]

    @pl.when(pl.program_id(0) == 0)
    def _():
        gain = gain_ref[0:1, :]

        def norm(i, carry):
            at = pl.ds(pl.multiple_of(i * STEP, STEP), STEP)
            x = x_ref[at, :].astype(F32)
            scale = lax.rsqrt(jnp.mean(x * x, axis=-1, keepdims=True) + EPSILON)
            n1_ref[at, :] = (x * scale * gain).astype(BF16)
            return carry

        lax.fori_loop(0, rows // STEP, norm, 0)
        xh = xh_ref[...].astype(F32)
        scale = lax.rsqrt(jnp.mean(xh * xh, axis=-1, keepdims=True) + EPSILON)
        n1h_ref[...] = (xh * scale * gain).astype(BF16)

    weight = w_ref[...].reshape(n1_ref.shape[1], CB)

    half = rows // 4
    for i in range(4):
        part = dot(n1_ref[i * half : (i + 1) * half, :], weight).astype(BF16).astype(F32)
        e_ref[LEAD + i * half : LEAD + (i + 1) * half, :] = part
    halo = dot(n1h_ref[...], weight).astype(BF16).astype(F32)
    first = lax.broadcasted_iota(jnp.int32, (SUB, CB), 0) == 0
    e_ref[0:SUB, :] = jnp.zeros((SUB, CB), F32)
    for q in range(1, CONV):
        tile = e_ref[LEAD + rows - SUB * q : LEAD + rows - SUB * (q - 1), :]
        tile = pltpu.roll(tile, 1, 0)
        e_ref[LEAD - SUB * q : LEAD - SUB * (q - 1), :] = jnp.where(
            first, jnp.broadcast_to(halo[q - 1 : q, :], (SUB, CB)), tile
        )
    xb_ref[...] = e_ref[...].astype(BF16)

    def chunk(i, carry):
        base = pl.multiple_of(i * WIDE, WIDE)
        at = pl.ds(base, WIDE)
        mask = mask_ref[at, :]
        total = small_ref[4:5, :] + small_ref[0:1, :] * e_ref[pl.ds(base + LEAD, WIDE), :]
        for k in range(1, CONV):
            shifted = e_ref[pl.ds(base + LEAD - SUB * k, WIDE), :]
            total = total + (small_ref[k : k + 1, :] * mask[:, k : k + 1]) * shifted
        low = total.astype(BF16)
        xc_ref[at, :] = low
        rate, enter = gates(low, g_ref, small_ref)
        flag = mask[:, 0:1]
        decay, _, multiplier = decay_parts(rate, small_ref[7:8, :], flag)
        drive = multiplier * enter * low.astype(F32)
        abar = decay * (1.0 - flag)
        ab_ref[at, :] = abar
        drive_ref[at, :] = drive
        product, state = carry
        for t in range(WIDE // SUB):
            a = abar[t * SUB : (t + 1) * SUB, :]
            product = product * a
            state = state * a + drive[t * SUB : (t + 1) * SUB, :]
        return product, state

    start = (jnp.ones((SUB, CB), F32), jnp.zeros((SUB, CB), F32))
    product, state = lax.fori_loop(0, rows // WIDE, chunk, start)
    tot_ref[0:SUB, :] = product
    tot_ref[SUB : 2 * SUB, :] = state
    whole_p, whole_s = product[0:1, :], state[0:1, :]
    for s in range(1, SUB):
        whole_s = whole_s * product[s : s + 1, :] + state[s : s + 1, :]
        whole_p = whole_p * product[s : s + 1, :]
    tot_ref[2 * SUB : 2 * SUB + 1, :] = whole_p
    tot_ref[2 * SUB + 1 : 2 * SUB + 2, :] = whole_s
    tot_ref[2 * SUB + 2 : 3 * SUB, :] = jnp.zeros((SUB - 2, CB), F32)


def front(x, x_halo, gain, recur_blocks, gate_pair, small, mask):
    rows, width = x.shape
    lru = gate_pair.shape[0]
    devices, per = recur_blocks.shape[0], width // recur_blocks.shape[0]
    col = lambda r: pl.BlockSpec((r, CB), lambda j: (0, j))
    return pl.pallas_call(
        front_kernel,
        grid=(lru // CB,),
        in_specs=[
            once((rows, width), lambda j: (0, 0)),
            once(x_halo.shape, lambda j: (0, 0)),
            once((1, width), lambda j: (0, 0)),
            pl.BlockSpec((devices, per, CB), lambda j: (0, j, 0)),
            pl.BlockSpec((CB, 2 * HEAD), lambda j: (j, 0)),
            col(SUB),
            once(mask.shape, lambda j: (0, 0)),
        ],
        out_specs=[
            once((rows, width), lambda j: (0, 0)),
            col(rows + LEAD), col(rows), col(rows), col(rows), col(3 * SUB),
            once(x_halo.shape, lambda j: (0, 0)),
        ],
        out_shape=[
            jax.ShapeDtypeStruct((rows, width), BF16),
            jax.ShapeDtypeStruct((rows + LEAD, lru), BF16),
            jax.ShapeDtypeStruct((rows, lru), BF16),
            jax.ShapeDtypeStruct((rows, lru), F32),
            jax.ShapeDtypeStruct((rows, lru), F32),
            jax.ShapeDtypeStruct((3 * SUB, lru), F32),
            jax.ShapeDtypeStruct(x_halo.shape, BF16),
        ],
        scratch_shapes=[pltpu.VMEM((rows + LEAD, CB), F32)],
        compiler_params=params(),
        cost_estimate=cost(33),
        name="front",
    )(x, x_halo, gain, recur_blocks, gate_pair, small, mask)


def branch_kernel(n_ref, w_ref, out_ref):
    out_ref[...] = dot(n_ref[...], w_ref[...].reshape(n_ref.shape[1], CB)).astype(BF16)


def branch(n1, bundle, lru):
    rows, width = n1.shape
    devices, steps = bundle.shape[0], lru // CB
    own = width // devices
    return pl.pallas_call(
        branch_kernel,
        grid=(lru // CB,),
        in_specs=[
            once((rows, width), lambda j: (0, 0)),
            pl.BlockSpec((devices, own, CB), lambda j: (0, j, 0)),
        ],
        out_specs=pl.BlockSpec((rows, CB), lambda j: (0, j)),
        out_shape=jax.ShapeDtypeStruct((rows, lru), BF16),
        compiler_params=params(),
        cost_estimate=cost(8),
        name="branch",
    )(n1, bundle)


def mix_kernel(*refs, pieces):
    ab_ref, drive_ref, yp_ref, x_ref, w0_ref, w1_ref, w2_ref, w3_ref, tot_ref, gain_ref = refs[:10]
    piece_refs = refs[10 : 10 + pieces]
    h_ref, z_ref, x1_ref, n2_ref, ent_ref, state_ref, piece_ref = refs[-7:]
    rows = ab_ref.shape[0]

    @pl.when(pl.program_id(0) == 0)
    def _():
        for k, ref in enumerate(piece_refs):
            piece_ref[k * SUB : (k + 1) * SUB, :] = ref[...]
        enter = fold_before(piece_ref)
        for s in range(SUB):
            ent_ref[s : s + 1, :] = enter
            enter = tot_ref[s : s + 1, :] * enter + tot_ref[SUB + s : SUB + s + 1, :]
        state_ref[...] = ent_ref[...]

    def tiles(i, state):
        at = pl.ds(pl.multiple_of(i * 2 * SUB, 2 * SUB), 2 * SUB)
        a, d = ab_ref[at, :], drive_ref[at, :]
        one = a[:SUB, :] * state + d[:SUB, :]
        two = a[SUB:, :] * one + d[SUB:, :]
        h = jnp.concatenate([one, two], axis=0)
        h_ref[at, :] = h.astype(BF16)
        z_ref[at, :] = (h * gelu_value(yp_ref[at, :].astype(F32))).astype(BF16)
        return two

    state_ref[...] = lax.fori_loop(0, rows // (2 * SUB), tiles, state_ref[...])
    z = z_ref[...]
    mixed = [dot(z, w[...].reshape(z.shape[1], CB)) for w in (w0_ref, w1_ref, w2_ref, w3_ref)]
    x1 = x_ref[...].astype(F32) + jnp.concatenate(mixed, axis=1)
    x1_ref[...] = x1
    scale = lax.rsqrt(jnp.mean(x1 * x1, axis=-1, keepdims=True) + EPSILON)
    n2_ref[...] = (x1 * scale * gain_ref[0:1, :]).astype(BF16)


def out_blocks(bundle, lru, width):
    devices = bundle.shape[0]
    own, ahead = lru // devices, (lru // CB) * (width // devices) // (lru // devices)
    return [
        once((devices, own, CB), lambda i, c=c: (0, ahead + c, 0)) for c in range(width // CB)
    ]


def mix(abar, drive, yp, x, bundle, tot, pieces, gain):
    rows, lru = abar.shape
    width = x.shape[1]
    weights = out_blocks(bundle, lru, width)
    block = 256
    row = lambda w: pl.BlockSpec((block, w), lambda i: (i, 0))
    whole = lambda a: once(a.shape, lambda i: (0, 0))
    return pl.pallas_call(
        functools.partial(mix_kernel, pieces=len(pieces)),
        grid=(rows // block,),
        in_specs=[
            row(lru), row(lru), row(lru), row(width),
            *weights, whole(tot), whole(gain), *[whole(piece) for piece in pieces],
        ],
        out_specs=[row(lru), row(lru), row(width), row(width), pl.BlockSpec((SUB, lru), lambda i: (0, 0))],
        out_shape=[
            jax.ShapeDtypeStruct((rows, lru), BF16),
            jax.ShapeDtypeStruct((rows, lru), BF16),
            jax.ShapeDtypeStruct((rows, width), F32),
            jax.ShapeDtypeStruct((rows, width), BF16),
            jax.ShapeDtypeStruct((SUB, lru), F32),
        ],
        scratch_shapes=[
            pltpu.VMEM((SUB, lru), F32), pltpu.VMEM((SUB * len(pieces), lru), F32),
        ],
        compiler_params=params(),
        cost_estimate=cost(15),
        name="mix",
    )(abar, drive, yp, x, *[bundle] * len(weights), tot, gain, *pieces)


def mlp_kernel(*refs, begins, ends):
    n_ref, g_ref, gate_ref, up_ref, d0_ref, d1_ref, d2_ref, d3_ref = refs[:8]
    refs = refs[8:]
    if not begins:
        acc_in_ref, dx_in_ref, _, _ = refs[:4]
        refs = refs[4:]
    if ends:
        x1_hbm, gain_ref, out_ref, dx_ref, do_ref, gg_ref = refs[:6]
        refs = refs[6:]
    else:
        acc_ref, dx_ref = refs[:2]
        refs = refs[2:]
    gu_mine_ref, gu_other_ref, down_mine_ref, down_other_ref = refs[:4]
    nt_ref, mm_ref, dl_ref, wt_ref, dt_ref = refs[4:9]
    if ends:
        acc_ref, x1_ref, x1_sem = refs[9:12]
    rows, width = n_ref.shape
    step = TALL
    j = pl.program_id(0)

    @pl.when(j == 0)
    def _():
        nt_ref[...] = n_ref[...].T
        if begins:
            acc_ref[...] = jnp.zeros_like(acc_ref)
            dx_ref[...] = jnp.zeros_like(dx_ref)
        else:
            acc_ref[...] = acc_in_ref[...]
            dx_ref[...] = dx_in_ref[...]

    own = gate_ref.shape[1] * CB // FB
    for p in range(FB // CB):
        here = slice(p * own, (p + 1) * own)
        wt_ref[:, p * CB : (p + 1) * CB] = gate_ref[:, here, :].reshape(width, CB)
        wt_ref[:, FB + p * CB : FB + (p + 1) * CB] = up_ref[:, here, :].reshape(width, CB)
    for c, ref in enumerate((d0_ref, d1_ref, d2_ref, d3_ref)):
        dt_ref[:, c * CB : (c + 1) * CB] = ref[...].reshape(FB, CB)

    def part(i, carry):
        at = pl.ds(pl.multiple_of(i * step, step), step)
        n, g = n_ref[at, :], g_ref[at, :]
        both = dot(n, wt_ref[...])
        gate_act, slope = gelu_parts(both[:, :FB])
        up = both[:, FB:]
        mm = (gate_act * up).astype(BF16)
        mm_ref[at, :] = mm
        grad = dot_t(g, dt_ref[...])
        dl_ref[at, :FB] = (grad * up * slope).astype(BF16)
        dl_ref[at, FB:] = (grad * gate_act).astype(BF16)
        acc_ref[at, :] += dot(mm, dt_ref[...])
        dx_ref[at, :] += dot_t(dl_ref[at, :], wt_ref[...])
        return carry

    lax.fori_loop(0, rows // step, part, 0, unroll=True)
    core = parity()
    per = gu_mine_ref.shape[1] // 2
    split(core, dot(nt_ref[...], dl_ref[:, :FB]), gu_mine_ref, gu_other_ref, slice(0, per))
    split(core, dot(nt_ref[...], dl_ref[:, FB:]), gu_mine_ref, gu_other_ref, slice(per, 2 * per))
    downs = halves(core, t_dot(mm_ref[...], g_ref[...]), down_mine_ref.shape[0])
    for owned, ref in zip(downs, (down_mine_ref, down_other_ref)):
        rows_own = owned.shape[1]
        ref[:, :rows_own, :] = owned[:, :, :FB]
        third = rows_own // 3
        for p in range(3):
            ref[:, rows_own:, p * CB : (p + 1) * CB] = owned[:, p * third : (p + 1) * third, FB:]

    if ends:

        @pl.when(j == pl.num_programs(0) - 1)
        def _():
            gain = gain_ref[0:1, :]

            def fetch(i):
                at = pl.ds(pl.multiple_of(i * STEP, STEP), STEP)
                slot = lax.rem(i, 2)
                return pltpu.make_async_copy(x1_hbm.at[at], x1_ref.at[slot], x1_sem.at[slot])

            fetch(0).start()

            def close(i, total):
                at = pl.ds(pl.multiple_of(i * STEP, STEP), STEP)

                @pl.when(i + 1 < rows // STEP)
                def _():
                    fetch(i + 1).start()

                fetch(i).wait()
                x1 = x1_ref[lax.rem(i, 2)]
                out_ref[at, :] = (x1 + acc_ref[at, :]).astype(BF16)
                scale = lax.rsqrt(jnp.mean(x1 * x1, axis=-1, keepdims=True) + EPSILON)
                q = x1 * scale
                dn = dx_ref[at, :]
                w = dn * gain
                inner = jnp.mean(w * q, axis=-1, keepdims=True)
                dx = g_ref[at, :].astype(F32) + scale * (w - q * inner)
                dx_ref[at, :] = dx
                do_ref[at, :] = dx.astype(BF16)
                return total + jnp.sum(dn * q, axis=0, keepdims=True)

            gg_ref[...] = jnp.broadcast_to(
                lax.fori_loop(0, rows // STEP, close, jnp.zeros((1, width), F32)), gg_ref.shape
            )


def mlp(n2, g, bundle, hidden, start, count, before=None, close=None):
    rows, width = n2.shape
    devices, steps = bundle.shape[0], hidden // FB
    own, per = width // devices, hidden // devices
    group = FB // per
    whole = lambda s: once(s, lambda j: (0, 0))
    lines = own * (FB // CB)
    gate = pl.BlockSpec((devices, lines, CB), lambda j: (0, start + j, 0))
    up = pl.BlockSpec((devices, lines, CB), lambda j: (0, steps + start + j, 0))
    downs = [
        pl.BlockSpec((group, per, CB), lambda j, c=c: (start + j, 2 * steps * lines // per + c, 0))
        for c in range(width // CB)
    ]
    pair = pl.BlockSpec((devices // 2, 2 * own, FB), lambda j: (0, j, 0))
    lines_down = per * width // FB
    half = pl.BlockSpec((group // 2, lines_down, FB), lambda j: (start + j, 0, 0))
    operands = [n2, g, bundle, bundle, *[bundle] * len(downs)]
    in_specs = [whole(n2.shape), whole(g.shape), gate, up, *downs]
    shape_f = jax.ShapeDtypeStruct((rows, width), F32)
    shape_b = jax.ShapeDtypeStruct((rows, width), BF16)
    aliases = {}
    if before is not None:
        operands += before
        in_specs += [whole(shape_f.shape)] * 2 + [pl.BlockSpec(memory_space=pl.ANY)] * 2
    if close is not None:
        operands += close
        in_specs += [pl.BlockSpec(memory_space=pl.ANY), whole(close[1].shape)]
        outs = [shape_b, shape_f, shape_b, jax.ShapeDtypeStruct((SUB, width), F32)]
    else:
        outs = [shape_f, shape_f]
    out_specs = [whole(shape.shape) for shape in outs]
    if before is not None:
        aliases = {10: len(outs) + 2, 11: len(outs) + 3}
    gu = jax.ShapeDtypeStruct((devices // 2, 2 * own * count, FB), BF16)
    down = jax.ShapeDtypeStruct((devices // 2, lines_down, FB), BF16)
    return pl.pallas_call(
        functools.partial(mlp_kernel, begins=before is None, ends=close is not None),
        grid=(count,),
        in_specs=in_specs,
        out_specs=out_specs + [pair, pair, half, half],
        out_shape=outs + [gu, gu, down, down],
        scratch_shapes=[
            pltpu.VMEM((width, rows), BF16),
            pltpu.VMEM((rows, FB), BF16),
            pltpu.VMEM((rows, 2 * FB), BF16),
            pltpu.VMEM((width, 2 * FB), BF16),
            pltpu.VMEM((FB, width), BF16),
        ]
        + (
            [
                pltpu.VMEM((rows, width), F32),
                pltpu.VMEM((2, STEP, width), F32),
                pltpu.SemaphoreType.DMA((2,)),
            ]
            if close is not None
            else []
        ),
        input_output_aliases=aliases,
        compiler_params=params(),
        cost_estimate=cost(20 * count),
        name="mlp",
    )(*operands)


def turn_kernel(
    do_ref, w0_ref, w1_ref, w2_ref, w3_ref, yp_ref, h_ref, ab_ref, tot_ref,
    dh_ref, dyp_ref, back_ref,
    dz_ref, w_ref,
):
    rows, width = do_ref.shape

    @pl.when(pl.program_id(0) == 0)
    def _():
        for c, ref in enumerate((w0_ref, w1_ref, w2_ref, w3_ref)):
            w_ref[:, c * CB : (c + 1) * CB] = ref[...].reshape(w_ref.shape[0], CB)

    weight = w_ref[pl.ds(pl.multiple_of(pl.program_id(0) * CB, CB), CB), :]
    half = rows // 4
    for i in range(4):
        dz_ref[i * half : (i + 1) * half, :] = dot_t(do_ref[i * half : (i + 1) * half, :], weight)

    def chunk(i, carry):
        base = pl.multiple_of((rows // WIDE - 1 - i) * WIDE, WIDE)
        at = pl.ds(base, WIDE)
        dz = dz_ref[at, :]
        act, slope = gelu_parts(yp_ref[at, :].astype(F32))
        dh = dz * act
        dh_ref[at, :] = dh
        dyp_ref[at, :] = (dz * h_ref[at, :].astype(F32) * slope).astype(BF16)
        abar = ab_ref[at, :]
        leave = carry
        for t in reversed(range(WIDE // SUB)):
            here = slice(t * SUB, (t + 1) * SUB)
            leave = abar[here, :] * (dh[here, :] + leave)
        return leave

    leave = lax.fori_loop(0, rows // WIDE, chunk, jnp.zeros((SUB, CB), F32))
    back_ref[0:SUB, :] = leave
    whole = leave[SUB - 1 : SUB, :]
    for s in reversed(range(SUB - 1)):
        whole = whole * tot_ref[s : s + 1, :] + leave[s : s + 1, :]
    back_ref[SUB : SUB + 1, :] = tot_ref[2 * SUB : 2 * SUB + 1, :]
    back_ref[SUB + 1 : SUB + 2, :] = whole
    back_ref[SUB + 2 : 2 * SUB, :] = jnp.zeros((SUB - 2, CB), F32)


def turn(do1, bundle, yp, h, abar, tot):
    rows, width = do1.shape
    lru = abar.shape[1]
    weights = out_blocks(bundle, lru, width)
    col = lambda r: pl.BlockSpec((r, CB), lambda j: (0, j))
    return pl.pallas_call(
        turn_kernel,
        grid=(lru // CB,),
        in_specs=[
            once((rows, width), lambda j: (0, 0)),
            *weights,
            col(rows), col(rows), col(rows), col(3 * SUB),
        ],
        out_specs=[col(rows), col(rows), col(2 * SUB)],
        out_shape=[
            jax.ShapeDtypeStruct((rows, lru), F32),
            jax.ShapeDtypeStruct((rows, lru), BF16),
            jax.ShapeDtypeStruct((2 * SUB, lru), F32),
        ],
        scratch_shapes=[pltpu.VMEM((rows, CB), F32), pltpu.VMEM((lru, width), BF16)],
        compiler_params=params(),
        cost_estimate=cost(15),
        name="turn",
    )(do1, *[bundle] * len(weights), yp, h, abar, tot)


def side_kernel(
    n_ref, dyp_ref, w_ref, z_ref, do_ref,
    both_ref, dn_ref,
    nt_ref,
):
    @pl.when(pl.program_id(0) == 0)
    def _():
        nt_ref[...] = n_ref[...].T
        dn_ref[...] = jnp.zeros_like(dn_ref)

    j = pl.program_id(0)
    width, block = n_ref.shape[1], dyp_ref.shape[1]
    own = w_ref.shape[1] * CB // block
    columns = pl.ds(pl.multiple_of(j * block, block), block)
    devices = both_ref.shape[0]
    both_ref[:, :own, columns] = dot(nt_ref[...], dyp_ref[...]).astype(BF16).reshape(devices, own, block)
    for p in range(block // CB):
        weight = w_ref[:, p * own : (p + 1) * own, :].reshape(width, CB)
        dn_ref[...] += dot_t(dyp_ref[:, p * CB : (p + 1) * CB], weight)
    half = devices // 2
    there = pl.ds(pl.multiple_of(j * half, half), half)
    out = t_dot(z_ref[...], do_ref[...]).astype(BF16).reshape(half, block // half, width)
    both_ref[there, own : 2 * own, :width] = out[:, :own, :]
    both_ref[there, own : own + own // 2, width:] = out[:, own:, : width // 2]
    both_ref[there, own + own // 2 : 2 * own, width:] = out[:, own:, width // 2 :]


def side(n1, dyp, weight, z, do1, devices):
    rows, width = n1.shape
    lru = dyp.shape[1]
    block = lru // 2
    both = (devices, 2 * (width // devices), lru)
    whole = once((rows, width), lambda j: (0, 0))
    col = pl.BlockSpec((rows, block), lambda j: (0, j))
    return pl.pallas_call(
        side_kernel,
        grid=(lru // block,),
        in_specs=[
            whole, col,
            pl.BlockSpec((devices, block // CB * (width // devices), CB), lambda j: (0, j, 0)),
            col, whole,
        ],
        out_specs=[once(both, lambda j: (0, 0, 0)), whole],
        out_shape=[
            jax.ShapeDtypeStruct(both, BF16),
            jax.ShapeDtypeStruct((rows, width), F32),
        ],
        scratch_shapes=[pltpu.VMEM((width, rows), BF16)],
        compiler_params=params(),
        cost_estimate=cost(16),
        name="side",
    )(n1, dyp, weight, z, do1)


def rear_kernel(*refs, pieces):
    dh_ref, xc_ref, ab_ref, h_ref, ent_ref, xb_ref, g_ref, small_ref, mask_ref, back_ref, tot_ref = refs[:11]
    piece_refs = refs[11 : 11 + pieces]
    dxb_ref, dg_ref, sum_ref, ret_ref, cin_ref, dxc_ref, dl_ref, piece_ref = refs[-8:]
    rows = dh_ref.shape[0]
    for k, ref in enumerate(piece_refs):
        piece_ref[k * SUB : (k + 1) * SUB, :] = ref[...]
    neg_soft = small_ref[7:8, :]

    leave = fold_after(piece_ref)
    for s in reversed(range(SUB)):
        cin_ref[s : s + 1, :] = leave
        leave = tot_ref[s : s + 1, :] * leave + back_ref[s : s + 1, :]

    def chunk(i, carry):
        leave, sums = carry
        base = pl.multiple_of((rows // rows - 1 - i) * rows, rows)
        at = pl.ds(base, rows)
        mask = mask_ref[at, :]
        flag = mask[:, 0:1]
        low = xc_ref[at, :]
        conv = low.astype(F32)
        rate, enter = gates(low, g_ref, small_ref)
        decay, inverse, multiplier = decay_parts(rate, neg_soft, flag)
        abar = ab_ref[at, :]
        dh = dh_ref[at, :]
        parts = []
        for t in reversed(range(rows // SUB)):
            here = slice(t * SUB, (t + 1) * SUB)
            delta = dh[here, :] + leave
            leave = abar[here, :] * delta
            parts.append(delta)
        delta = jnp.concatenate(parts[::-1], axis=0)
        now = h_ref[at, :].astype(F32)
        before_at = pl.ds(pl.multiple_of(jnp.maximum(base - 2 * SUB, 0), 2 * SUB), 2 * SUB)
        before = h_ref[before_at, :].astype(F32)[SUB:, :]
        before = jnp.where(base == 0, ent_ref[...], before)
        prior = jnp.concatenate([before, now[: rows - SUB, :]], axis=0)
        gated = delta * enter
        dla = (1.0 - flag) * decay * (delta * prior - gated * conv * (decay * inverse))
        by_rate = dla * rate
        dr = neg_soft * by_rate * (1.0 - rate)
        scaled = delta * multiplier
        di = scaled * conv * enter * (1.0 - enter)
        drl, dil = dr.astype(BF16), di.astype(BF16)
        one = jnp.concatenate([drl[:, :HEAD], dil[:, :HEAD]], axis=1)
        two = jnp.concatenate([drl[:, HEAD:], dil[:, HEAD:]], axis=1)
        dl_ref[at, : 2 * HEAD] = one
        dl_ref[at, 2 * HEAD :] = two
        through = jnp.concatenate(
            [dot_t(one, g_ref[:HEAD, :]), dot_t(two, g_ref[HEAD:, :])], axis=1
        )
        dxc = scaled * enter + through
        dxc_ref[at, :] = dxc
        fold = lambda v: functools.reduce(
            lambda a, b: a + b, [v[t * SUB : (t + 1) * SUB, :] for t in range(rows // SUB)]
        )
        new = [fold(dr), fold(di), fold(by_rate), fold(dxc)]
        for k in range(CONV):
            more = 2 * SUB * (k % 2)
            lines = pl.ds(pl.multiple_of(base + LEAD - SUB * (k + k % 2), 2 * SUB), rows + more)
            shift = xb_ref[lines, :].astype(F32)[more // 2 : more // 2 + rows, :]
            term = dxc * shift
            if k:
                term = term * mask[:, k : k + 1]
            new.append(fold(term))
        return leave, tuple(a + b for a, b in zip(sums, new))

    zero = jnp.zeros((SUB, CB), F32)
    _, sums = lax.fori_loop(0, rows // rows, chunk, (cin_ref[...], (zero,) * 8))
    for r, value in enumerate(sums):
        sum_ref[r : r + 1, :] = jnp.sum(value, axis=0, keepdims=True)

    for q in range(CONV - 1):
        tile = dxc_ref[q * SUB : (q + 1) * SUB, :]
        dxc_ref[rows + q * SUB : rows + (q + 1) * SUB, :] = pltpu.roll(tile, SUB - 1, 0)
    for q in range(1, CONV):
        back = jnp.zeros((1, CB), F32)
        for k in range(q, CONV):
            t = (k - q) * SUB
            back = back + small_ref[k : k + 1, :] * mask_ref[t : t + 1, k : k + 1] * dxc_ref[t : t + 1, :]
        ret_ref[q - 1 : q, :] = back
    ret_ref[CONV - 1 :, :] = jnp.zeros((SUB - CONV + 1, CB), F32)

    def spread(i, carry):
        base = pl.multiple_of(i * rows, rows)
        total = small_ref[0:1, :] * dxc_ref[pl.ds(base, rows), :]
        for k in range(1, CONV):
            at = pl.ds(base + SUB * k, rows)
            total = total + (small_ref[k : k + 1, :] * mask_ref[at, k : k + 1]) * dxc_ref[at, :]
        dxb_ref[pl.ds(base, rows), :] = total.astype(BF16)
        return carry

    lax.fori_loop(0, rows // rows, spread, 0)
    dg_ref[:HEAD, :] = t_dot(xc_ref[:, :HEAD], dl_ref[:, : 2 * HEAD])
    dg_ref[HEAD:, :] = t_dot(xc_ref[:, HEAD:], dl_ref[:, 2 * HEAD :])


def rear(dh, xc, abar, h, ent, xb, gate_pair, small, mask, back, tot, pieces, start, count, before=()):
    rows, lru = dh.shape
    col = lambda r: pl.BlockSpec((r, CB), lambda j: (0, start + j))
    pair = pl.BlockSpec((CB, 2 * HEAD), lambda j: (start + j, 0))
    operands = [dh, xc, abar, h, ent, xb, gate_pair, small, mask, back, tot, *pieces, *before]
    return pl.pallas_call(
        functools.partial(rear_kernel, pieces=len(pieces)),
        grid=(count,),
        in_specs=[
            col(rows), col(rows), col(rows), col(rows), col(SUB), col(rows + LEAD), pair, col(SUB),
            once(mask.shape, lambda j: (0, 0)),
            col(2 * SUB), col(3 * SUB),
        ]
        + [col(SUB)] * len(pieces)
        + [pl.BlockSpec(memory_space=pl.ANY)] * len(before),
        out_specs=[col(rows), pair, col(SUB), col(SUB)],
        out_shape=[
            jax.ShapeDtypeStruct((rows, lru), BF16),
            jax.ShapeDtypeStruct((lru, 2 * HEAD), F32),
            jax.ShapeDtypeStruct((SUB, lru), F32),
            jax.ShapeDtypeStruct((SUB, lru), F32),
        ],
        scratch_shapes=[
            pltpu.VMEM((SUB, CB), F32),
            pltpu.VMEM((rows + LEAD, CB), F32),
            pltpu.VMEM((rows, 4 * HEAD), BF16),
            pltpu.VMEM((SUB * len(pieces), CB), F32),
        ],
        input_output_aliases={len(operands) - len(before) + i: i for i in range(len(before))},
        compiler_params=params(),
        cost_estimate=cost(7 * count),
        name="rear",
    )(*operands)


def with_edge(dxb_ref, ret_ref):
    rows, width = dxb_ref.shape
    lastly = lax.broadcasted_iota(jnp.int32, (SUB, width), 0) == SUB - 1
    tail = dxb_ref[rows - 4 * SUB :, :].astype(F32)
    tiles = [tail[:SUB, :]]
    for q in reversed(range(1, CONV)):
        tile = tail[(4 - q) * SUB : (5 - q) * SUB, :]
        tiles.append(tile + jnp.where(lastly, ret_ref[q - 1 : q, :], 0.0))
    return jnp.concatenate(tiles, axis=0).astype(BF16)


def weigh_kernel(n_ref, nh_ref, d_ref, ret_ref, dp_ref, mine_ref, other_ref, nt_ref):
    @pl.when(pl.program_id(0) == 0)
    def _():
        nt_ref[...] = n_ref[...].T

    width = n_ref.shape[1]
    core = parity()
    per = width // (2 * mine_ref.shape[0])
    edge = jnp.concatenate([ret_ref[...], jnp.zeros_like(ret_ref)], axis=0).astype(BF16)
    grad = dot(nt_ref[...], d_ref[...]) + t_dot(nh_ref[...], edge)
    split(core, grad, mine_ref, other_ref, slice(0, per))
    devices, lines, wide = dp_ref.shape
    pair = jnp.concatenate([dp_ref[...], jnp.zeros_like(dp_ref)], axis=1)
    split(core, pair.reshape(devices * 2 * lines, wide), mine_ref, other_ref, slice(per, per + 2 * lines))


def weigh(n1, n1_halo, dxb, ret, dpair):
    rows, width = n1.shape
    lru = dxb.shape[1]
    devices, per = GROUPS, width // GROUPS
    col = lambda r: pl.BlockSpec((r, CB), lambda j: (0, j))
    lines = lru // devices // (lru // CB)
    dpair = dpair.reshape(devices, lru // devices, 2 * HEAD)
    bundle = pl.BlockSpec((devices // 2, per + 2 * lines, CB), lambda j: (0, 0, j))
    shape = jax.ShapeDtypeStruct((devices // 2, per + 2 * lines, lru), BF16)
    return pl.pallas_call(
        weigh_kernel,
        grid=(lru // CB,),
        in_specs=[
            once(n1.shape, lambda j: (0, 0)), once(n1_halo.shape, lambda j: (0, 0)), col(rows), col(SUB),
            pl.BlockSpec((devices, lines, 2 * HEAD), lambda j: (0, j, 0)),
        ],
        out_specs=[bundle, bundle],
        out_shape=[shape, shape],
        scratch_shapes=[pltpu.VMEM((width, rows), BF16)],
        compiler_params=params(),
        cost_estimate=cost(8),
        name="weigh",
    )(n1, n1_halo, dxb, ret, dpair)


def last_kernel(d_ref, ret_ref, w_ref, dn_ref, x_ref, dx_ref, gain_ref, out_ref, wt_ref, e_ref):
    rows, width = x_ref.shape
    block = 256

    @pl.when(pl.program_id(0) == 0)
    def _():
        own = w_ref.shape[1] * CB // wt_ref.shape[1]
        for p in range(wt_ref.shape[1] // CB):
            here = slice(p * own, (p + 1) * own)
            wt_ref[:, p * CB : (p + 1) * CB] = w_ref[:, here, :].reshape(width, CB)

    x = x_ref[...].astype(F32)
    scale = lax.rsqrt(jnp.mean(x * x, axis=-1, keepdims=True) + EPSILON)
    q = x * scale
    e_ref[...] = d_ref[...]

    @pl.when(pl.program_id(0) == pl.num_programs(0) - 1)
    def _():
        e_ref[rows - 4 * SUB :, :] = with_edge(d_ref, ret_ref)

    dn = dn_ref[...] + dot_t(e_ref[...], wt_ref[...])
    w = dn * gain_ref[0:1, :]
    inner = jnp.mean(w * q, axis=-1, keepdims=True)
    out_ref[...] = (dx_ref[...] + scale * (w - q * inner)).astype(BF16)


def last(dxb, ret, recur_blocks, dn, x, dx1, gain):
    rows, lru = dxb.shape
    width = x.shape[1]
    devices, per = recur_blocks.shape[0], width // recur_blocks.shape[0]
    block = 256
    row = lambda w: pl.BlockSpec((block, w), lambda i: (i, 0))
    return pl.pallas_call(
        last_kernel,
        grid=(rows // block,),
        in_specs=[
            row(lru), once(ret.shape, lambda i: (0, 0)),
            once((devices, per * (lru // CB), CB), lambda i: (0, 0, 0)),
            row(width), row(width), row(width), once(gain.shape, lambda i: (0, 0)),
        ],
        out_specs=row(width),
        out_shape=jax.ShapeDtypeStruct(x.shape, BF16),
        scratch_shapes=[pltpu.VMEM((width, lru), BF16), pltpu.VMEM((block, lru), BF16)],
        compiler_params=params(),
        cost_estimate=cost(11),
        name="last",
    )(dxb, ret, recur_blocks, dn, x, dx1, gain)


def interleave(values):
    return values.reshape((SUB, values.shape[0] // SUB) + values.shape[1:]).swapaxes(0, 1).reshape(values.shape)


def uninterleave(values):
    return values.reshape((values.shape[0] // SUB, SUB) + values.shape[1:]).swapaxes(0, 1).reshape(values.shape)


def exchange(value):
    core = lax.axis_index("seq") % 2
    came = permute(value, 0, 1)
    pair = jnp.concatenate(
        [
            jnp.where(core == 0, value, came),
            jnp.where(core == 0, came, value),
            jnp.zeros((SUB - 2 * value.shape[0],) + value.shape[1:], value.dtype),
        ],
        axis=0,
    )
    count = lax.axis_size("seq") // 2
    return [pair] + [permute(pair, 0, 2 * k) for k in range(1, count)]


def fold_before(piece_ref):
    place = lax.axis_index("seq")
    at = place // 2
    value = jnp.zeros((1, piece_ref.shape[1]), F32)
    for k in range(piece_ref.shape[0] // SUB):
        rows = piece_ref[pl.ds(pl.multiple_of((at ^ k) * SUB, SUB), SUB), :]
        value = jnp.where(2 * k < place, rows[0:1, :] * value + rows[1:2, :], value)
        value = jnp.where(2 * k + 1 < place, rows[2:3, :] * value + rows[3:4, :], value)
    return value


def fold_after(piece_ref):
    place = lax.axis_index("seq")
    at = place // 2
    value = jnp.zeros((1, piece_ref.shape[1]), F32)
    for k in reversed(range(piece_ref.shape[0] // SUB)):
        rows = piece_ref[pl.ds(pl.multiple_of((at ^ k) * SUB, SUB), SUB), :]
        value = jnp.where(2 * k + 1 > place, rows[2:3, :] * value + rows[3:4, :], value)
        value = jnp.where(2 * k > place, rows[0:1, :] * value + rows[1:2, :], value)
    return value


def pack_kernel(*refs, layout):
    outs = refs[len(refs) - len({at[0] for at in layout}) :]
    for out, row, source, column in layout:
        block = refs[source][:, column : column + CB]
        outs[out][row : row + block.shape[0], :] = block


def pack(*bundles):
    layout, sources, shapes = [], [], []
    for out, arrays in enumerate(bundles):
        row = 0
        for array in arrays:
            for column in range(0, array.shape[1], CB):
                layout.append((out, row, len(sources), column))
                row += array.shape[0]
            sources.append(array)
        shapes.append(jax.ShapeDtypeStruct((row, CB), BF16))
    return pl.pallas_call(
        functools.partial(pack_kernel, layout=tuple(layout)),
        out_shape=shapes,
        compiler_params=params(),
        cost_estimate=cost(2),
        name="pack",
    )(*sources)


def place_kernel(*refs, slots):
    pieces, out, sems = refs[: len(slots)], refs[len(slots)], refs[len(slots) + 1]
    at_dp, place = lax.axis_index("dp"), lax.axis_index("seq")
    at, core = place // 2, place % 2
    lines = out.shape[1]
    here = pl.ds(pl.multiple_of(pl.program_id(0) * lines, lines), lines)
    copies = []
    for ref, (dp_step, core_step, steps) in zip(pieces, slots):
        for i, k in enumerate(steps):
            owner = ((at_dp ^ dp_step) * 4 + (at ^ k)) * 2 + (core ^ core_step)
            copies.append(
                pltpu.make_async_copy(ref.at[i, here], out.at[owner], sems.at[len(copies)])
            )
    for copy in copies:
        copy.start()
    for copy in copies:
        copy.wait()


def place(pieces, time):
    arrays = [piece[0] for piece in pieces]
    rows = arrays[0].shape[1]
    steps = 4
    return pl.pallas_call(
        functools.partial(place_kernel, slots=tuple(piece[1:] for piece in pieces)),
        grid=(steps,),
        in_specs=[pl.BlockSpec(memory_space=pl.ANY)] * len(arrays),
        out_specs=pl.BlockSpec((GROUPS, rows // steps, CB), lambda i: (0, i, 0)),
        out_shape=jax.ShapeDtypeStruct((GROUPS, rows, CB), BF16),
        scratch_shapes=[pltpu.SemaphoreType.DMA((GROUPS,))],
        compiler_params=params(),
        cost_estimate=cost(time),
        name="place",
    )(*arrays)


def spread_line(bundle):
    count = lax.axis_size("seq") // 2
    return jnp.stack([bundle] + [permute(bundle, 0, 2 * k) for k in range(1, count)], axis=0)


def spread_near(line):
    return permute(line, 1, 0), permute(line, 2, 0)


def spread_far(near):
    half = near[0].shape[0] // 2
    return permute(near[0][:half], 2, 0), permute(near[1][half:], 1, 0)


def to_core(pieces):
    return tuple(permute(piece, 0, 1) for piece in pieces)


def placed(line, near, far, line_c, near_c, far_c, time):
    every, low, high = (0, 1, 2, 3), (0, 1), (2, 3)
    return place(
        [
            (line, 0, 0, every), (near[0], 1, 0, every), (near[1], 2, 0, every),
            (far[0], 3, 0, low), (far[1], 3, 0, high),
            (line_c, 0, 1, every), (near_c[0], 1, 1, every), (near_c[1], 2, 1, every),
            (far_c[0], 3, 1, low), (far_c[1], 3, 1, high),
        ],
        time,
    )


def gather(value):
    return lax.all_gather(value, AXES, axis=0, tiled=False)


def scatter(value):
    return lax.psum_scatter(value, AXES, scatter_dimension=0, tiled=True).astype(F32)


def regroup(full, sections):
    fold = full.shape[0] // GROUPS
    if fold == 1:
        return full
    parts, at = [], 0
    for blocks, rows in sections:
        part = full[:, at : at + blocks * rows].reshape(GROUPS, fold, blocks, rows, CB)
        parts.append(part.swapaxes(1, 2).reshape(GROUPS, blocks * fold * rows, CB))
        at += blocks * rows
    return jnp.concatenate(parts, axis=1)


def joined(mine, other):
    return jnp.stack([mine, other], axis=1).reshape((GROUPS,) + mine.shape[1:])


def permute(value, dp_step, seq_step):
    n_dp, n_seq = lax.axis_size("dp"), lax.axis_size("seq")
    route = [
        (a * n_seq + b, (a ^ dp_step) * n_seq + (b ^ seq_step))
        for a in range(n_dp)
        for b in range(n_seq)
    ]
    return lax.ppermute(value, AXES, route)


def total(parts):
    return functools.reduce(lambda a, b: a + b, [part.astype(F32) for part in parts])


def after(values, *others):
    return lax.optimization_barrier((values, others))[0]


def pick(value, index, axis=0):
    return lax.dynamic_index_in_dim(value, index, axis, keepdims=False)


def meet_core(halves):
    mine, came = halves
    n_dp, at = lax.axis_size("dp"), lax.axis_index("dp")
    shape = (n_dp, mine.shape[0] // n_dp) + mine.shape[1:]
    mine, came = mine.reshape(shape), came.reshape(shape)
    return [total([pick(mine, at ^ m), pick(came, at ^ m)]).astype(BF16) for m in range(n_dp)]


def send_far(parts):
    half = parts[3].shape[0] // 2
    return permute(parts[3][:half], 1, 0), permute(parts[3][half:], 2, 0)


def meet_far(parts, far):
    half = parts[3].shape[0] // 2
    one = jnp.concatenate(
        [parts[1][:half], total([parts[1][half:], far[1]]).astype(BF16)], axis=0
    )
    two = jnp.concatenate(
        [total([parts[2][:half], far[0]]).astype(BF16), parts[2][half:]], axis=0
    )
    return one, two


def send_near(pair):
    return permute(pair[0], 1, 0), permute(pair[1], 2, 0)


def meet_near(own, near):
    at, count = lax.axis_index("seq") // 2, own.shape[0]
    parts = (own,) + tuple(near)
    return [total([pick(part, at ^ k) for part in parts]).astype(BF16) for k in range(count)]


def send_line(parts):
    return [permute(parts[k], 0, 2 * k) for k in range(1, len(parts))]


def meet_line(parts, came):
    return total([parts[0]] + list(came))


def column_blocks(shard, width):
    rows, columns = shard.shape
    return jnp.concatenate([shard[:, c : c + width] for c in range(0, columns, width)], axis=0)


def from_column_blocks(blocks, rows):
    return jnp.concatenate(
        [blocks[r : r + rows] for r in range(0, blocks.shape[0], rows)], axis=1
    )


def mask_table(flags, tail):
    rows = flags.shape[0]
    extended = jnp.concatenate([tail, flags])
    columns = [flags]
    valid = jnp.ones_like(flags)
    for k in range(1, CONV):
        valid = valid * (1.0 - extended[CONV - k : CONV - k + rows])
        columns.append(valid)
    table = jnp.stack(columns, axis=1)
    run = rows // SUB
    tiles = table.reshape(SUB, run, CONV)
    ahead = jnp.concatenate(
        [tiles[1:, : CONV - 1], jnp.zeros((1, CONV - 1, CONV), F32)], axis=0
    )
    tiles = jnp.concatenate([tiles, ahead], axis=1)
    table = tiles.swapaxes(0, 1).reshape((run + CONV - 1) * SUB, CONV)
    return jnp.pad(table, ((0, 0), (0, SUB - CONV)))


def back_edge(ret):
    count = lax.axis_size("seq")
    return lax.ppermute(ret, "seq", [(i + 1, i) for i in range(count - 1)])


def undo_down(value, width):
    rows = value.shape[-2] * FB // width
    rest = value[..., rows:, :]
    rest = jnp.concatenate([rest[..., p * CB : (p + 1) * CB] for p in range(3)], axis=-2)
    return jnp.concatenate([value[..., :rows, :], rest], axis=-1)


def undo_out(value, width):
    own = value.shape[-2]
    rest = value[..., width:]
    rest = jnp.concatenate([rest[..., : own // 2, :], rest[..., own // 2 :, :]], axis=-1)
    return jnp.concatenate([value[..., :width], rest], axis=-2)


def vector_sums(sums, gain2_part, mine):
    devices = lax.axis_size("dp") * lax.axis_size("seq")
    sums = sums.reshape(SUB, devices, mine).swapaxes(0, 1).reshape(devices, SUB * mine)
    return jnp.concatenate([sums, gain2_part[0].reshape(devices, -1)], axis=1)


def plain_back(
    grads_m, do1, full1, full2, yp, h, abar, tot, n1, n1_halo, z,
    xc, ent, xb, gate_pair, small, mask, x, dx1, gain1, gain2_part, mine,
):
    width, lru = n1.shape[1], abar.shape[1]
    dh, dyp, back = turn(do1, full2, yp, h, abar, tot)
    behind = exchange(back[SUB : SUB + 2])
    both, dn1 = side(n1, dyp, full2, z, do1, GROUPS)
    dxb, dpair, sums, ret = rear(
        dh, xc, abar, h, ent, xb, gate_pair, small, mask, back, tot, behind, 0, lru // CB
    )
    last_mine, last_other = weigh(n1, n1_halo, dxb, ret, dpair)
    tokens_grad = last(dxb, back_edge(ret), full1, dn1, x, dx1, gain1)
    gu_mine, gu_other, down_mine, down_other = grads_m
    own = width // GROUPS
    gu = joined(gu_mine, gu_other).reshape(GROUPS, -1, 2, own, FB)
    gate, up = (gu[:, :, i].swapaxes(1, 2).reshape(width, -1) for i in range(2))
    bundle = joined(last_mine, last_other)
    vectors = vector_sums(sums, gain2_part, mine)
    grads = (
        scatter(gate), scatter(up),
        scatter(undo_down(joined(down_mine, down_other), width).reshape(-1, width)),
        scatter(both[:, :own].reshape(width, lru)),
        scatter(undo_out(both[:, own:], width).reshape(lru, width)),
        scatter(bundle[:, :own].reshape(width, lru)),
        scatter(dpair.astype(BF16)),
    )
    return grads, scatter(vectors).reshape(-1), tokens_grad


def staged_back(
    grads_m, do1, full1, full2, yp, h, abar, tot, n1, n1_halo, z,
    xc, ent, xb, gate_pair, small, mask, x, dx1, gain1, gain2_part, mine,
):
    devices, per = GROUPS, n1.shape[1] // GROUPS
    lru = abar.shape[1]
    blocks = lru // CB
    gu_mine, gu_other, down_mine, down_other = grads_m
    sent_gu, sent_down = permute(gu_other, 0, 1), permute(down_other, 0, 1)
    dh, dyp, back = turn(do1, full2, yp, h, abar, tot)
    sent_gu, sent_down, back = after((sent_gu, sent_down, back))
    parts_m = [
        jnp.concatenate(pair, axis=1)
        for pair in zip(meet_core((gu_mine, sent_gu)), meet_core((down_mine, sent_down)))
    ]
    parts_m, dyp = after((parts_m, dyp))
    far_m = send_far(parts_m)
    both, dn1 = side(n1, dyp, full2, z, do1, devices)
    far_m, dn1 = after((far_m, dn1))
    sum_b = lax.psum_scatter(both, AXES, scatter_dimension=0, tiled=False)
    pair_m = meet_far(parts_m, far_m)
    pair_m, dh = after((pair_m, dh))
    near_m = send_near(pair_m)
    behind = exchange(after(back[SUB : SUB + 2], pair_m))
    dxb, dpair, sums, ret = rear(
        dh, xc, abar, h, ent, xb, gate_pair, small, mask, back, tot, behind, 0, blocks
    )
    last_mine, last_other = weigh(n1, n1_halo, dxb, ret, dpair)
    near_m, last_mine, last_other, ret = after((near_m, last_mine, last_other, ret))
    line_m = meet_near(parts_m[0], near_m)
    sent_m = send_line(line_m)
    ret = back_edge(ret)
    flat = vector_sums(sums, gain2_part, mine)
    lines = mine // blocks
    flat = jnp.pad(flat, ((0, 0), (0, lines * lru - flat.shape[1])))
    flat = flat.astype(BF16).reshape(devices // 2, 2, lines, lru)
    core = lax.axis_index("seq") % 2
    last_mine = lax.dynamic_update_slice(last_mine, pick(flat, core, 1), (0, per + lines, 0))
    last_other = lax.dynamic_update_slice(last_other, pick(flat, 1 - core, 1), (0, per + lines, 0))
    sent_l = permute(last_other, 0, 1)
    parts_l = meet_core((last_mine, sent_l))
    far_l = send_far(parts_l)
    parts_l, line_m, dxb = after((parts_l, line_m, dxb))
    tokens_grad = last(dxb, ret, full1, dn1, x, dx1, gain1)
    far_l, tokens_grad = after((far_l, tokens_grad))
    pair_l = meet_far(parts_l, far_l)
    near_l = send_near(pair_l)
    near_l, sent_m = after((near_l, sent_m))
    sum_m = meet_line(line_m, sent_m)
    count_m = gu_mine.shape[1]
    gu = sum_m[:count_m].reshape(-1, 2, per, FB)
    mlp_gate_grad = gu[:, 0].swapaxes(0, 1).reshape(per, -1)
    mlp_up_grad = gu[:, 1].swapaxes(0, 1).reshape(per, -1)
    mlp_down_grad = undo_down(sum_m[count_m:], n1.shape[1])
    line_l = meet_near(parts_l[0], near_l)
    sent_line_l = send_line(line_l)
    sum_b = sum_b.astype(F32)
    gelu_branch_grad, mixer_out_grad = sum_b[:per], undo_out(sum_b[per:], n1.shape[1])
    sent_line_l = after(sent_line_l, (gelu_branch_grad, mixer_out_grad))
    bundle = meet_line(line_l, sent_line_l)
    recur_in_grad = bundle[:per]
    pair = bundle[per : per + lines].reshape(lines, blocks, CB).swapaxes(0, 1).reshape(mine, CB)
    flat = bundle[per + lines :].reshape(-1)
    grads = (
        mlp_gate_grad, mlp_up_grad, mlp_down_grad, gelu_branch_grad, mixer_out_grad, recur_in_grad, pair,
    )
    return grads, flat, tokens_grad


def on_device(
    tokens, seg_starts, cotangent, recur_in, gelu_branch, mixer_out, conv_weight, conv_bias,
    rate_gate, input_gate, rate_bias, input_bias, decay_param, mixer_gain, mlp_gate, mlp_up,
    mlp_down, mlp_gain,
):
    rows, width = tokens.shape
    devices = lax.axis_size("dp") * lax.axis_size("seq")
    count = lax.axis_size("seq")
    lru = recur_in.shape[1]
    mine = conv_bias.shape[0]
    share = mixer_gain.shape[0]

    per = recur_in.shape[0]
    blocks = lru // CB
    across = lambda array, rows: jnp.pad(array, ((0, rows - array.shape[0]), (0, CB - array.shape[1])))
    vectors = jnp.concatenate(
        [
            across(
                jnp.concatenate(
                    [conv_weight, conv_bias[None], rate_bias[None], input_bias[None], decay_param[None]],
                    axis=0,
                ),
                SUB,
            ),
            across(jnp.stack([mixer_gain, mlp_gain], axis=0), SUB),
        ],
        axis=0,
    )
    hidden = mlp_gate.shape[1]
    flags = seg_starts.astype(F32)
    pair = jnp.concatenate([rate_gate, input_gate], axis=1)
    lag = CONV - 1
    tail = jnp.concatenate(
        [tokens[rows - lag :], jnp.pad(flags[rows - lag :].astype(BF16), (0, width - lag))[None]], axis=0
    )
    send_on = lambda value: lax.ppermute(value, "seq", [(i, i + 1) for i in range(count - 1)])
    if staged():
        (first,) = pack([recur_in, pair, vectors])
        line1 = spread_line(first)
        second, third = pack([gelu_branch, mixer_out], [mlp_gate, mlp_up, mlp_down])
        tail = send_on(after(tail, first))
        line1, second, tail = after((line1, second, tail))
        near1 = spread_near(line1)
        line2 = spread_line(second)
        far1 = spread_far(near1)
        line1, near1_b, line2 = after((line1, near1, line2))
        full3 = gather(after(third, near1_b))
        line1_c, near1_c = to_core((line1,))[0], to_core(near1_b)
        far1, line1_c, near1_c, line2 = after((far1, line1_c, near1_c, line2))
        far1_c = to_core(far1)
        far1_c, line2 = after((far1_c, line2))
        near2 = spread_near(line2)
        full1 = placed(line1, near1, far1, line1_c, near1_c, far1_c, 4)
    else:
        full1 = gather(jnp.concatenate([column_blocks(recur_in, CB), pair, vectors], axis=0))
        tail = send_on(tail)
    x_halo, flag_tail = tail[:lag], tail[lag, :lag].astype(F32)
    mask = mask_table(flags, flag_tail)
    pair_at = per * blocks
    raw = full1
    gate_pair = raw[:, pair_at : pair_at + mine].reshape(lru, 2 * HEAD)
    small = raw[:, pair_at + mine : pair_at + mine + SUB, :mine].astype(F32)
    small = small.swapaxes(0, 1).reshape(SUB, lru)
    gain1, gain2 = (
        raw[:, pair_at + mine + SUB + i, :share].astype(F32).reshape(1, width) for i in range(2)
    )
    small = jnp.concatenate([small[:7], -RATE_SCALE * jax.nn.softplus(-small[7:8])], axis=0)
    full1 = regroup(raw, [(blocks, per)])

    x = interleave(tokens)
    g = interleave(cotangent)
    x_halo = jnp.pad(x_halo[::-1], ((0, 16 - (CONV - 1)), (0, 0)))

    n1, xb, xc, abar, drive, tot, n1_halo = front(x, x_halo, gain1, full1, gate_pair, small, mask)
    ahead = tot[2 * SUB : 2 * SUB + 2]
    if staged():
        near2, ahead = after((near2, ahead))
        far2 = spread_far(near2)
        line2_c, near2_c = to_core((line2,))[0], to_core(near2)
        ahead = exchange(ahead)
        far2, line2_c, near2_c, ahead = after((far2, line2_c, near2_c, ahead))
        far2_c = to_core(far2)
        full2 = placed(line2, near2, far2, line2_c, near2_c, far2_c, 5)
    else:
        ahead = exchange(ahead)
        second = jnp.concatenate([column_blocks(gelu_branch, CB), column_blocks(mixer_out, CB)], axis=0)
        full2 = regroup(gather(second), [(blocks, per), (width // CB, mine)])
    yp = branch(n1, full2, lru)
    h, z, x1, n2, ent = mix(abar, drive, yp, x, full2, tot, ahead, gain2)
    if not staged():
        third = [column_blocks(array, CB) for array in (mlp_gate, mlp_up, mlp_down)]
        full3 = regroup(
            gather(jnp.concatenate(third)),
            [(hidden // CB, per), (hidden // CB, per), (width // CB, hidden // devices)],
        )
    out, dx1, do1, gain2_part, *grads_m = mlp(
        n2, g, full3, hidden, 0, hidden // FB, None, [x1, gain2]
    )
    grads, flat, tokens_grad = (staged_back if staged() else plain_back)(
        grads_m, do1, full1, full2, yp, h, abar, tot, n1, n1_halo, z,
        xc, ent, xb, gate_pair, small, mask, x, dx1, gain1, gain2_part, mine,
    )
    mlp_gate_grad, mlp_up_grad, mlp_down_grad, gelu_branch_grad, mixer_out_grad, recur_in_grad, pair = grads
    by_gain = sum(
        jnp.sum(weight.astype(F32) * grad, axis=1)
        for weight, grad in ((recur_in, recur_in_grad), (gelu_branch, gelu_branch_grad))
    )
    gain1_grad = by_gain / mixer_gain.astype(F32)
    row = lambda r: flat[r * mine : (r + 1) * mine]
    decay_grad = RATE_SCALE * jax.nn.sigmoid(-decay_param.astype(F32)) * row(2)
    gain_at = SUB * mine
    return (
        uninterleave(out),
        uninterleave(tokens_grad),
        recur_in_grad,
        gelu_branch_grad,
        mixer_out_grad,
        flat[4 * mine : 8 * mine].reshape(CONV, mine),
        row(3),
        pair[:, :HEAD],
        pair[:, HEAD:],
        row(0),
        row(1),
        decay_grad,
        gain1_grad,
        mlp_gate_grad,
        mlp_up_grad,
        mlp_down_grad,
        flat[gain_at : gain_at + share],
    )


def solution(mesh):
    both, alone = P(AXES, None), P(AXES)
    across = P(None, AXES)
    return jax.shard_map(
        on_device,
        mesh=mesh,
        in_specs=(
            both, alone, both, both, both, both, across, alone, both, both, alone, alone, alone,
            alone, both, both, both, alone,
        ),
        out_specs=(
            both, both, both, both, both, across, alone, both, both, alone, alone, alone, alone,
            both, both, both, alone,
        ),
        check_vma=False,
    )
```
